512 devices in a mesh: ctx: 64 (over z_lo, x, y), head: 8 (over z_hi, core).
Axes of the slice: x: 4, y: 8, z: 8 (z_hi: 4, z_lo: 2; z = z_hi * 2 + z_lo), core: 2. Of those that a mesh axis runs over, the one named last changes fastest.
Arguments:
- queries: bfloat16 [32768, 4096], P(('ctx', 'head')), may hold values from -6 to 6
- stacked_keys: bfloat16 [32768, 1024], P(('ctx', 'head')), may hold values from -6 to 6
- stacked_values: bfloat16 [32768, 1024], P(('ctx', 'head')), may hold values from -6 to 6
- output_gradient: bfloat16 [32768, 4096], P(('ctx', 'head')), may hold values from -6 to 6
- doc_ids: int32 [32768], P('ctx'), may hold values from 0 to 127, never falling along the last dimension, each value on 1 to 1024 neighbouring positions
Outputs:
- attended: bfloat16 [32768, 4096], P(('ctx', 'head'))
- query_grad: bfloat16 [32768, 4096], P(('ctx', 'head'))
- key_grad: bfloat16 [32768, 1024], P(('ctx', 'head'))
- value_grad: bfloat16 [32768, 1024], P(('ctx', 'head'))
The draws below stay inside these ranges and needn't reach their ends.
Inputs may be any that keep to these rules, and one draw needn't show every extreme that they name: `doc_ids`: document ids never fall along the sequence; each document has 1 to 1024 tokens and one has exactly 1024.
All inputs are finite; a program needn't handle non-finite values.
Results may differ from the reference program's by a relative error of at most 0.012.
The reference program's roundings to bfloat16 on the way count: a program that leaves them out, or rounds other values in their place, can miss the bound.
Values may be sent and summed in bfloat16 or wider, within the bound.
A program may use at most 64 MiB of HBM per device.

```python
import math
import jax
import jax.numpy as jnp
import numpy as np
from jax import lax

QUERY_HEADS = 32
KEY_VALUE_HEADS = 8
HEAD_SIZE = 128
CONTEXT_TOKENS = 512
DOCUMENT_LIMIT = 1024
PACKED_TOKENS = 32768
N_CTX = 64


def draw_queries(key, part):
    key = jax.random.fold_in(key, 1)
    final_output = jnp.clip(jax.random.normal(key, (PACKED_TOKENS, QUERY_HEADS * HEAD_SIZE), jnp.float32), -6.0, 6.0)
    return final_output.astype(jnp.bfloat16)


def draw_stacked_keys(key, part):
    key = jax.random.fold_in(key, 2)
    final_output = jnp.clip(jax.random.normal(key, (PACKED_TOKENS, KEY_VALUE_HEADS * HEAD_SIZE), jnp.float32), -6.0, 6.0)
    return final_output.astype(jnp.bfloat16)


def block_scale(rng, extent, pieces, low, largest):
    loudness = 1.0
    for axis_at, blocks in pieces:
        steps = jax.random.uniform(jax.random.fold_in(jax.random.fold_in(rng, 6), axis_at), (blocks,), jnp.float32, low / len(pieces), largest / len(pieces))
        loudness = loudness * jnp.repeat(jnp.exp(steps), extent[axis_at] // blocks).reshape((-1,) + (1,) * (len(extent) - 1 - axis_at))
    return loudness


def split_up(count, total, most, lean):
    weights = [(1 << 20) // math.isqrt(rank ** lean) + 1 for rank in range(2, count + 1)]
    rest, holding = total - most - (count - 1), [1] * (count - 1)
    while rest > 0:
        free = [i for i in range(count - 1) if holding[i] < most]
        pool, remaining = sum([weights[i] for i in free]), rest
        for i in free:
            more = min(most - holding[i], max(1, remaining * weights[i] // pool), rest)
            holding[i] = holding[i] + more
            rest = rest - more
    return np.array([most] + holding)


def uneven_parts(rng, number_of, total, most, slope):
    if number_of == 2:
        one = jax.random.randint(rng, (), max(1, total - most), min(most, total - 1) + 1)
        return jnp.stack([one, total - one])
    tallies = jnp.asarray(split_up(number_of, total, most, slope), jnp.int32)
    couples = (number_of - 1) // 2
    source_of, sink = tallies[1:1 + 2 * couples:2], tallies[2:2 + 2 * couples:2]
    margin = jnp.minimum(source_of - 1, most - sink)
    passed = jax.random.randint(jax.random.fold_in(rng, 1), (couples,), 0, 1 << 20) % (margin + 1)
    tallies = tallies.at[1:1 + 2 * couples:2].set(source_of - passed).at[2:2 + 2 * couples:2].set(sink + passed)
    return tallies[jax.random.permutation(jax.random.fold_in(rng, 2), number_of)]


def noise(rng, extent, width, most, split=(), kind=jnp.bfloat16):
    loudness = block_scale(rng, extent, split, -0.22, 0.18) if split else 1.0
    result = jax.random.normal(rng, extent, jnp.float32) * width * loudness
    return jnp.minimum(jnp.maximum(result, -most), most).astype(kind)


def setup_inputs(seed: int = 0) -> dict:
    arg_keys = jax.random.split(jax.random.key(seed), 6)
    queries = draw_queries(jax.random.fold_in(arg_keys[5], 71), 0)
    stacked_keys = draw_stacked_keys(jax.random.fold_in(arg_keys[5], 71), 0)
    stacked_values = noise(arg_keys[2], (PACKED_TOKENS, KEY_VALUE_HEADS * HEAD_SIZE), 1.0, 6.0, ((0, 512),))
    output_gradient = noise(arg_keys[3], (PACKED_TOKENS, QUERY_HEADS * HEAD_SIZE), 1.0, 6.0, ((0, 512),))
    doc_ids = jnp.searchsorted(jnp.cumsum(uneven_parts(arg_keys[4], 2 * N_CTX, PACKED_TOKENS, DOCUMENT_LIMIT, 2)), jnp.arange(PACKED_TOKENS), side="right").astype(jnp.int32)
    return dict(queries=queries, stacked_keys=stacked_keys, stacked_values=stacked_values, output_gradient=output_gradient, doc_ids=doc_ids)


def reference(queries, stacked_keys, stacked_values, output_gradient, doc_ids):
    group_width = QUERY_HEADS // KEY_VALUE_HEADS
    logit_scale = 1.0 / math.sqrt(HEAD_SIZE)
    visible_span = DOCUMENT_LIMIT + CONTEXT_TOKENS
    key_padding = jnp.concatenate([jnp.zeros((DOCUMENT_LIMIT, KEY_VALUE_HEADS * HEAD_SIZE), stacked_keys.dtype), stacked_keys], axis=0)
    value_padding = jnp.concatenate([jnp.zeros((DOCUMENT_LIMIT, KEY_VALUE_HEADS * HEAD_SIZE), stacked_values.dtype), stacked_values], axis=0)
    doc_pad = jnp.concatenate([jnp.full((DOCUMENT_LIMIT,), -1, jnp.int32), doc_ids.astype(jnp.int32)])
    offsets = jnp.arange(CONTEXT_TOKENS, dtype=jnp.int32)
    spread = jnp.arange(visible_span, dtype=jnp.int32)

    def block_step(carried, block_index):
        key_sum, value_sum = carried
        leading_row = (block_index * CONTEXT_TOKENS).astype(jnp.int32)
        query_tile = lax.dynamic_slice_in_dim(queries, leading_row, CONTEXT_TOKENS, 0).astype(jnp.float32).reshape(CONTEXT_TOKENS, KEY_VALUE_HEADS, group_width, HEAD_SIZE)
        output_grad_block = lax.dynamic_slice_in_dim(output_gradient, leading_row, CONTEXT_TOKENS, 0).astype(jnp.float32).reshape(CONTEXT_TOKENS, KEY_VALUE_HEADS, group_width, HEAD_SIZE)
        key_span = lax.dynamic_slice_in_dim(key_padding, leading_row, visible_span, 0).astype(jnp.float32).reshape(visible_span, KEY_VALUE_HEADS, HEAD_SIZE)
        value_span = lax.dynamic_slice_in_dim(value_padding, leading_row, visible_span, 0).astype(jnp.float32).reshape(visible_span, KEY_VALUE_HEADS, HEAD_SIZE)
        query_docs = lax.dynamic_slice_in_dim(doc_ids.astype(jnp.int32), leading_row, CONTEXT_TOKENS, 0)
        key_docs = lax.dynamic_slice_in_dim(doc_pad, leading_row, visible_span, 0)
        query_positions = leading_row + offsets
        key_positions = leading_row - DOCUMENT_LIMIT + spread
        allowed = (query_docs[:, None] == key_docs[None, :]) & (key_positions[None, :] <= query_positions[:, None])
        scores = jnp.einsum('tkgd,wkd->kgtw', query_tile, key_span) * logit_scale
        scores = jnp.where(allowed[None, None], scores, -jnp.inf)
        row_peak = lax.optimization_barrier(jnp.max(scores, axis=-1, keepdims=True))
        log_total = row_peak + jnp.log(lax.optimization_barrier(jnp.sum(jnp.exp(scores - row_peak), axis=-1, keepdims=True)))
        attention_probs = lax.optimization_barrier(jnp.exp(scores - log_total).astype(jnp.bfloat16)).astype(jnp.float32)
        attended = jnp.einsum('kgtw,wkd->tkgd', attention_probs, value_span).astype(jnp.bfloat16)
        attended_wide = lax.optimization_barrier(attended).astype(jnp.float32)
        dout_dot = jnp.transpose(lax.optimization_barrier(jnp.sum(attended_wide * output_grad_block, axis=-1)), (1, 2, 0))[..., None]
        dout_values = jnp.einsum('tkgd,wkd->kgtw', output_grad_block, value_span)
        score_gradient = lax.optimization_barrier((attention_probs * (dout_values - dout_dot)).astype(jnp.bfloat16)).astype(jnp.float32)
        query_grad = (logit_scale * jnp.einsum('kgtw,wkd->tkgd', score_gradient, key_span)).astype(jnp.bfloat16)
        key_portion = (logit_scale * jnp.einsum('pvsi,spvu->ipu', score_gradient, query_tile)).reshape(visible_span, KEY_VALUE_HEADS * HEAD_SIZE)
        value_portion = jnp.einsum('pvsi,spvu->ipu', attention_probs, output_grad_block).reshape(visible_span, KEY_VALUE_HEADS * HEAD_SIZE)
        key_sum = lax.dynamic_update_slice_in_dim(key_sum, lax.dynamic_slice_in_dim(key_sum, leading_row, visible_span, 0) + key_portion, leading_row, 0)
        value_sum = lax.dynamic_update_slice_in_dim(value_sum, lax.dynamic_slice_in_dim(value_sum, leading_row, visible_span, 0) + value_portion, leading_row, 0)
        return ((key_sum, value_sum), (attended.reshape(CONTEXT_TOKENS, QUERY_HEADS * HEAD_SIZE), query_grad.reshape(CONTEXT_TOKENS, QUERY_HEADS * HEAD_SIZE)))
    zero_gradients = jnp.zeros((DOCUMENT_LIMIT + PACKED_TOKENS, KEY_VALUE_HEADS * HEAD_SIZE), jnp.float32)
    (key_sum, value_sum), (attended, query_grad) = lax.scan(block_step, (zero_gradients, zero_gradients), jnp.arange(N_CTX, dtype=jnp.int32))
    return (attended.reshape(PACKED_TOKENS, QUERY_HEADS * HEAD_SIZE), query_grad.reshape(PACKED_TOKENS, QUERY_HEADS * HEAD_SIZE), key_sum[DOCUMENT_LIMIT:].astype(jnp.bfloat16), value_sum[DOCUMENT_LIMIT:].astype(jnp.bfloat16))
```

```python
import math

import jax
import jax.numpy as jnp
from jax import lax
from jax.experimental import pallas as pl
from jax.experimental.pallas import tpu as pltpu
from jax.sharding import PartitionSpec as P

D = 128
TOK = 64
SL = 128
BLK = 512
WIN = 1536
KEYS = 1152
GRP = 4
MESH = pl.DeviceIdType.MESH
SCALE = 1.0 / math.sqrt(D)
LOG2E = 1.4426950408889634


def nt(a, b):
    return lax.dot_general(a, b, (((1,), (1,)), ((), ())), preferred_element_type=jnp.float32)


def tn(a, b):
    return lax.dot_general(a, b, (((0,), (0,)), ((), ())), preferred_element_type=jnp.float32)


def kernel(
    q_ref, k_ref, v_ref, g_ref, doc_ref,
    att_ref, dq_ref, dk_ref, dv_ref,
    kv, qg, docw, startb, outb, acc, hsend, hrecv, osend,
    kv_send, kv_recv, qg_send, qg_recv, halo_send, halo_recv, doc_send, doc_recv, own_sem,
    out_send, out_recv, part_send, part_recv, grad_send, grad_recv,
):
    n_ctx = lax.axis_size("ctx")
    c = lax.axis_index("ctx")
    h = lax.axis_index("head")
    zh = h // 2
    core = lax.rem(h, 2)

    def head_dev(dz, dk):
        return lax.rem(zh + dz, 4) * 2 + lax.rem(core + dk, 2)

    def ctx_dev(dc):
        return lax.rem(c + dc + n_ctx, n_ctx)

    peers = [(0, 1), (1, 0), (1, 1), (3, 0), (3, 1), (2, 0), (2, 1)]

    own_row = pl.multiple_of(2 * BLK + h * TOK, TOK)
    col_q = pl.multiple_of(h * BLK, BLK)
    col_k = pl.multiple_of(h * D, D)
    tok_row = pl.multiple_of(core * TOK, TOK)
    for i, src in enumerate((k_ref, v_ref)):
        pltpu.make_async_copy(src.at[:, pl.ds(col_k, D)], kv.at[i, pl.ds(own_row, TOK)], kv_recv).start()
    for i, src in enumerate((q_ref, g_ref)):
        pltpu.make_async_copy(
            src.at[:, pl.ds(col_q, BLK)], qg.at[zh, i, pl.ds(tok_row, TOK)], qg_recv.at[zh]
        ).start()
    pltpu.make_async_copy(doc_ref, docw.at[2], own_sem).start()

    barrier = pltpu.get_barrier_semaphore()
    for dz, dk in peers:
        pl.semaphore_signal(barrier, inc=1, device_id=(c, head_dev(dz, dk)), device_id_type=MESH)
    for dc in (-2, -1, 1, 2):
        pl.semaphore_signal(barrier, inc=1, device_id=(ctx_dev(dc), h), device_id_type=MESH)
    pl.semaphore_wait(barrier, len(peers) + 4)

    for dz, dk in peers:
        p = head_dev(dz, dk)
        for i, src in enumerate((k_ref, v_ref)):
            pltpu.make_async_remote_copy(
                src_ref=src.at[:, pl.ds(pl.multiple_of(p * D, D), D)],
                dst_ref=kv.at[i, pl.ds(own_row, TOK)],
                send_sem=kv_send, recv_sem=kv_recv, device_id=(c, p), device_id_type=MESH,
            ).start()
    for dc in (1, 2):
        pltpu.make_async_remote_copy(
            src_ref=doc_ref, dst_ref=docw.at[2 - dc], send_sem=doc_send.at[dc - 1], recv_sem=doc_recv.at[dc - 1],
            device_id=(ctx_dev(dc), h), device_id_type=MESH,
        ).start()
    for dz, dk in peers:
        p = head_dev(dz, dk)
        for i, src in enumerate((q_ref, g_ref)):
            pltpu.make_async_remote_copy(
                src_ref=src.at[:, pl.ds(pl.multiple_of(p * BLK, BLK), BLK)],
                dst_ref=qg.at[zh, i, pl.ds(tok_row, TOK)],
                send_sem=qg_send.at[i], recv_sem=qg_recv.at[zh], device_id=(c, p), device_id_type=MESH,
            ).start()

    own_kv = kv.at[:, pl.ds(2 * BLK, BLK)]
    pltpu.make_async_copy(own_kv, own_kv, kv_recv).wait()
    for dc in (1, 2):
        pltpu.make_async_remote_copy(
            src_ref=own_kv, dst_ref=kv.at[:, pl.ds((2 - dc) * BLK, BLK)],
            send_sem=halo_send.at[dc - 1], recv_sem=halo_recv.at[dc - 1],
            device_id=(ctx_dev(dc), h), device_id_type=MESH,
        ).start()

    acc[...] = jnp.zeros_like(acc)
    pltpu.make_async_copy(doc_ref, docw.at[2], own_sem).wait()
    for dc in (1, 2):
        pltpu.make_async_copy(docw.at[2 - dc], docw.at[2 - dc], doc_recv.at[dc - 1]).wait()
    docs = jnp.concatenate([docw[0], docw[1], docw[2]], axis=1)
    lane = lax.broadcasted_iota(jnp.int32, (1, WIN), 1)
    docs = jnp.where(lane + (c - 2) * BLK >= 0, docs, -1)
    docs = jnp.broadcast_to(docs, (8, WIN))
    lane = lax.broadcasted_iota(jnp.int32, (8, WIN), 1)
    begins = jnp.where((lane == 0) | (docs != pltpu.roll(docs, 1, 1)), lane, 0)
    step = 1
    while step < WIN:
        begins = jnp.maximum(begins, jnp.where(lane >= step, pltpu.roll(begins, step, 1), 0))
        step *= 2
    for s in range(4):
        startb[s] = begins[:, 2 * BLK + s * SL : 2 * BLK + (s + 1) * SL]

    for dc in (1, 2):
        part = kv.at[:, pl.ds((2 - dc) * BLK, BLK)]
        pltpu.make_async_copy(part, part, halo_recv.at[dc - 1]).wait()

    def unit(j, carry):
        s = lax.rem(zh + jnp.where(j == 2, 3, jnp.where(j == 3, 2, j)), 4)
        pltpu.make_async_copy(qg.at[s], qg.at[s], qg_recv.at[s]).wait()
        first = pl.multiple_of(s * SL, SL)
        keys = kv[0, pl.ds(first, KEYS)]
        values = kv[1, pl.ds(first, KEYS)]
        q4 = jnp.concatenate([qg[s, 0, :, i * D : (i + 1) * D] for i in range(GRP)], axis=0)
        g4 = jnp.concatenate([qg[s, 1, :, i * D : (i + 1) * D] for i in range(GRP)], axis=0)
        start = startb[s][0:1]
        start = jnp.concatenate([start] * GRP, axis=1) - first
        scores = nt(keys, q4) * (SCALE * LOG2E)
        row = lax.broadcasted_iota(jnp.int32, (KEYS, GRP * SL), 0)
        column = lax.rem(lax.broadcasted_iota(jnp.int32, (1, GRP * SL), 1), SL) + 2 * BLK
        scores = jnp.where((row >= start) & (row <= column), scores, -jnp.inf)
        peak = jnp.max(scores, axis=0, keepdims=True)
        weights = jnp.exp2(scores - peak)
        total = jnp.sum(weights, axis=0, keepdims=True)
        weights = (weights * (1.0 / total)).astype(jnp.bfloat16)
        att = tn(values, weights).astype(jnp.bfloat16).astype(jnp.float32)
        g_t = jnp.transpose(g4.astype(jnp.float32))
        dot = jnp.sum(att * g_t, axis=0, keepdims=True)
        for i in range(GRP):
            outb[s, 0, :, i * D : (i + 1) * D] = jnp.transpose(att[:, i * D : (i + 1) * D]).astype(jnp.bfloat16)
        acc[1, pl.ds(first, KEYS)] += jnp.dot(weights, g4, preferred_element_type=jnp.float32)
        dscore = (weights.astype(jnp.float32) * (nt(values, g4) - dot)).astype(jnp.bfloat16)
        dq = tn(keys, dscore) * SCALE
        for i in range(GRP):
            outb[s, 1, :, i * D : (i + 1) * D] = jnp.transpose(dq[:, i * D : (i + 1) * D]).astype(jnp.bfloat16)
        acc[0, pl.ds(first, KEYS)] += jnp.dot(dscore, q4, preferred_element_type=jnp.float32)
        for i, dst in enumerate((att_ref, dq_ref)):
            for cc in range(2):
                piece = outb.at[s, i, pl.ds(cc * TOK, TOK)]
                there = dst.at[:, pl.ds(col_q, BLK)]

                @pl.when(2 * s + cc == h)
                def _():
                    pltpu.make_async_copy(piece, there, out_recv.at[i]).start()

                @pl.when(2 * s + cc != h)
                def _():
                    pltpu.make_async_remote_copy(
                        src_ref=piece, dst_ref=there, send_sem=out_send.at[i], recv_sem=out_recv.at[i],
                        device_id=(c, 2 * s + cc), device_id_type=MESH,
                    ).start()

        return carry

    lax.fori_loop(0, 4, unit, 0)

    for dc in (1, 2):
        rows = slice((2 - dc) * BLK, (3 - dc) * BLK)
        hsend[dc - 1, 0] = (acc[0, rows] * SCALE).astype(jnp.bfloat16)
        hsend[dc - 1, 1] = acc[1, rows].astype(jnp.bfloat16)
        pltpu.make_async_remote_copy(
            src_ref=hsend.at[dc - 1], dst_ref=hrecv.at[dc - 1],
            send_sem=part_send.at[dc - 1], recv_sem=part_recv.at[dc - 1],
            device_id=(ctx_dev(-dc), h), device_id_type=MESH,
        ).start()
    for dc in (1, 2):
        pltpu.make_async_copy(hrecv.at[dc - 1], hrecv.at[dc - 1], part_recv.at[dc - 1]).wait()
    for i in range(2):
        mine = acc[i, 2 * BLK :] * (SCALE if i == 0 else 1.0)
        osend[i] = (mine + hrecv[0, i].astype(jnp.float32) + hrecv[1, i].astype(jnp.float32)).astype(jnp.bfloat16)
    for i, dst in enumerate((dk_ref, dv_ref)):
        there = dst.at[:, pl.ds(col_k, D)]
        pltpu.make_async_copy(
            osend.at[i, pl.ds(pl.multiple_of(h * TOK, TOK), TOK)], there, grad_recv.at[i]
        ).start()
        for dz, dk in peers:
            p = head_dev(dz, dk)
            pltpu.make_async_remote_copy(
                src_ref=osend.at[i, pl.ds(pl.multiple_of(p * TOK, TOK), TOK)], dst_ref=there,
                send_sem=grad_send.at[i], recv_sem=grad_recv.at[i], device_id=(c, p), device_id_type=MESH,
            ).start()

    def drain(ref, sem):
        pltpu.make_async_copy(ref, ref, sem).wait()

    for i, dst in enumerate((att_ref, dq_ref)):
        drain(dst, out_recv.at[i])
    for i, dst in enumerate((dk_ref, dv_ref)):
        drain(dst, grad_recv.at[i])
    sent = len(peers) * TOK
    for i in range(2):
        drain(osend.at[i, pl.ds(0, sent)], grad_send.at[i])
        drain(att_ref.at[:, pl.ds(0, len(peers) * BLK)], out_send.at[i])
        drain(hsend.at[i], part_send.at[i])
        drain(own_kv, halo_send.at[i])
        drain(docw.at[i], doc_send.at[i])
    drain(kv.at[:, pl.ds(0, sent)], kv_send)
    for i in range(2):
        drain(att_ref.at[:, pl.ds(0, len(peers) * BLK)], qg_send.at[i])


def on_device(queries, stacked_keys, stacked_values, output_gradient, doc_ids):
    any_ref = pl.BlockSpec(memory_space=pl.ANY)
    dma = pltpu.SemaphoreType.DMA
    shapes = [jax.ShapeDtypeStruct(a.shape, a.dtype) for a in (queries, queries, stacked_keys, stacked_values)]
    return pl.pallas_call(
        kernel,
        out_shape=shapes,
        in_specs=[any_ref] * 5,
        out_specs=[any_ref] * 4,
        scratch_shapes=[
            pltpu.VMEM((2, WIN, D), jnp.bfloat16),
            pltpu.VMEM((4, 2, SL, BLK), jnp.bfloat16),
            pltpu.VMEM((3, 1, BLK), jnp.int32),
            pltpu.VMEM((4, 8, SL), jnp.int32),
            pltpu.VMEM((4, 2, SL, BLK), jnp.bfloat16),
            pltpu.VMEM((2, WIN, D), jnp.float32),
            pltpu.VMEM((2, 2, BLK, D), jnp.bfloat16),
            pltpu.VMEM((2, 2, BLK, D), jnp.bfloat16),
            pltpu.VMEM((2, BLK, D), jnp.bfloat16),
            dma, dma, dma((2,)), dma((4,)), dma((2,)), dma((2,)), dma((2,)), dma((2,)), dma,
            dma((2,)), dma((2,)), dma((2,)), dma((2,)), dma((2,)), dma((2,)),
        ],
        compiler_params=pltpu.CompilerParams(
            collective_id=0, has_side_effects=True, vmem_limit_bytes=48 * 2**20
        ),
    )(queries, stacked_keys, stacked_values, output_gradient, doc_ids.reshape(1, -1))


def solution(mesh):
    tokens = P(("ctx", "head"), None)
    return jax.shard_map(
        on_device, mesh=mesh, in_specs=(tokens,) * 4 + (P("ctx"),), out_specs=(tokens,) * 4, check_vma=False
    )
```

```python
import math

import jax
import jax.numpy as jnp
from jax import lax
from jax.experimental import pallas as pl
from jax.experimental.pallas import tpu as pltpu
from jax.sharding import PartitionSpec as P

D = 128
TOK = 64
SL = 128
BLK = 512
HALF = 256
WIN = 1536
KEYS = 1152
GRP = 4
MESH = pl.DeviceIdType.MESH
SCALE = 1.0 / math.sqrt(D)
LOG2E = 1.4426950408889634


def nt(a, b):
    return lax.dot_general(a, b, (((1,), (1,)), ((), ())), preferred_element_type=jnp.float32)


def tn(a, b):
    return lax.dot_general(a, b, (((0,), (0,)), ((), ())), preferred_element_type=jnp.float32)


def kernel(
    q_ref, k_ref, v_ref, g_ref, doc_ref,
    att_ref, dq_ref, dk_ref, dv_ref,
    kv, qg, docw, startb, outb, acc, hsend, hrecv, osend,
    kv_send, kv_recv, qg_send, qg_recv, halo_send, halo_recv, doc_send, doc_recv, own_sem,
    out_send, out_recv, part_send, part_recv, grad_send, grad_recv,
):
    n_ctx = lax.axis_size("ctx")
    c = lax.axis_index("ctx")
    h = lax.axis_index("head")
    zh = h // 2
    core = lax.rem(h, 2)

    def head_dev(dz, dk):
        return lax.rem(zh + dz, 4) * 2 + lax.rem(core + dk, 2)

    def ctx_dev(dc):
        return lax.rem(c + dc + n_ctx, n_ctx)

    peers = [(0, 1), (1, 0), (1, 1), (3, 0), (3, 1), (2, 0), (2, 1)]

    own_row = pl.multiple_of(2 * BLK + h * TOK, TOK)
    col_q = pl.multiple_of(h * BLK, BLK)
    col_k = pl.multiple_of(h * D, D)
    tok_row = pl.multiple_of(core * TOK, TOK)
    for i, src in enumerate((k_ref, v_ref)):
        pltpu.make_async_copy(src.at[:, pl.ds(col_k, D)], kv.at[i, pl.ds(own_row, TOK)], kv_recv.at[i]).start()
    for i, src in enumerate((q_ref, g_ref)):
        pltpu.make_async_copy(
            src.at[:, pl.ds(col_q, BLK)], qg.at[zh, i, pl.ds(tok_row, TOK)], qg_recv.at[zh]
        ).start()
    pltpu.make_async_copy(doc_ref, docw.at[2], own_sem).start()

    barrier = pltpu.get_barrier_semaphore()
    for dz, dk in peers:
        pl.semaphore_signal(barrier, inc=1, device_id=(c, head_dev(dz, dk)), device_id_type=MESH)
    for dc in (-1, 1):
        pl.semaphore_signal(barrier, inc=1, device_id=(ctx_dev(dc), h), device_id_type=MESH)
    pl.semaphore_wait(barrier, len(peers) + 2)

    for i, src in enumerate((k_ref, v_ref)):
        for dz, dk in peers:
            p = head_dev(dz, dk)
            pltpu.make_async_remote_copy(
                src_ref=src.at[:, pl.ds(pl.multiple_of(p * D, D), D)],
                dst_ref=kv.at[i, pl.ds(own_row, TOK)],
                send_sem=kv_send, recv_sem=kv_recv.at[i], device_id=(c, p), device_id_type=MESH,
            ).start()

    after, before = (ctx_dev(1), h), (ctx_dev(-1), h)

    def pass_on(src, dst, send_sem, recv_sem, to=after):
        pltpu.make_async_remote_copy(
            src_ref=src, dst_ref=dst, send_sem=send_sem, recv_sem=recv_sem, device_id=to, device_id_type=MESH
        ).start()

    def arrived(ref, sem):
        pltpu.make_async_copy(ref, ref, sem).wait()

    def chunk(i, r, block):
        return kv.at[i, pl.ds(block * BLK + r * HALF, HALF)]

    for dz, dk in peers[:5]:
        p = head_dev(dz, dk)
        for i, src in enumerate((q_ref, g_ref)):
            pltpu.make_async_remote_copy(
                src_ref=src.at[:, pl.ds(pl.multiple_of(p * BLK, BLK), BLK)],
                dst_ref=qg.at[zh, i, pl.ds(tok_row, TOK)],
                send_sem=qg_send.at[i], recv_sem=qg_recv.at[zh], device_id=(c, p), device_id_type=MESH,
            ).start()

    pass_on(doc_ref, docw.at[1], doc_send.at[0], doc_recv.at[0])
    for i in range(2):
        arrived(kv.at[i, pl.ds(2 * BLK, BLK)], kv_recv.at[i])
        for r in range(2):
            pass_on(chunk(i, r, 2), chunk(i, r, 1), halo_send.at[0, i, r], halo_recv.at[0, i, r])

    for dz, dk in peers[5:]:
        p = head_dev(dz, dk)
        for i, src in enumerate((q_ref, g_ref)):
            pltpu.make_async_remote_copy(
                src_ref=src.at[:, pl.ds(pl.multiple_of(p * BLK, BLK), BLK)],
                dst_ref=qg.at[zh, i, pl.ds(tok_row, TOK)],
                send_sem=qg_send.at[i], recv_sem=qg_recv.at[zh], device_id=(c, p), device_id_type=MESH,
            ).start()

    arrived(docw.at[1], doc_recv.at[0])
    pass_on(docw.at[1], docw.at[0], doc_send.at[1], doc_recv.at[1])
    for i in range(2):
        for r in range(2):
            arrived(chunk(i, r, 1), halo_recv.at[0, i, r])
            pass_on(chunk(i, r, 1), chunk(i, r, 0), halo_send.at[1, i, r], halo_recv.at[1, i, r])

    acc[...] = jnp.zeros_like(acc)
    pltpu.make_async_copy(doc_ref, docw.at[2], own_sem).wait()
    arrived(docw.at[0], doc_recv.at[1])
    docs = jnp.concatenate([docw[0], docw[1], docw[2]], axis=1)
    lane = lax.broadcasted_iota(jnp.int32, (1, WIN), 1)
    docs = jnp.where(lane + (c - 2) * BLK >= 0, docs, -1)
    docs = jnp.broadcast_to(docs, (8, WIN))
    lane = lax.broadcasted_iota(jnp.int32, (8, WIN), 1)
    begins = jnp.where((lane == 0) | (docs != pltpu.roll(docs, 1, 1)), lane, 0)
    step = 1
    while step < WIN:
        begins = jnp.maximum(begins, jnp.where(lane >= step, pltpu.roll(begins, step, 1), 0))
        step *= 2
    for s in range(4):
        startb[s] = begins[:, 2 * BLK + s * SL : 2 * BLK + (s + 1) * SL]

    for i in range(2):
        for r in range(2):
            arrived(chunk(i, r, 0), halo_recv.at[1, i, r])

    def unit(j, carry):
        s = lax.rem(zh + jnp.where(j == 2, 3, jnp.where(j == 3, 2, j)), 4)
        pltpu.make_async_copy(qg.at[s], qg.at[s], qg_recv.at[s]).wait()
        first = pl.multiple_of(s * SL, SL)
        keys = kv[0, pl.ds(first, KEYS)]
        values = kv[1, pl.ds(first, KEYS)]
        q4 = jnp.concatenate([qg[s, 0, :, i * D : (i + 1) * D] for i in range(GRP)], axis=0)
        g4 = jnp.concatenate([qg[s, 1, :, i * D : (i + 1) * D] for i in range(GRP)], axis=0)
        start = startb[s][0:1]
        start = jnp.concatenate([start] * GRP, axis=1) - first
        scores = nt(keys, q4) * (SCALE * LOG2E)
        row = lax.broadcasted_iota(jnp.int32, (KEYS, GRP * SL), 0)
        column = lax.rem(lax.broadcasted_iota(jnp.int32, (1, GRP * SL), 1), SL) + 2 * BLK
        scores = jnp.where((row >= start) & (row <= column), scores, -jnp.inf)
        peak = jnp.max(scores, axis=0, keepdims=True)
        weights = jnp.exp2(scores - peak)
        total = jnp.sum(weights, axis=0, keepdims=True)
        weights = (weights * (1.0 / total)).astype(jnp.bfloat16)
        att = tn(values, weights).astype(jnp.bfloat16).astype(jnp.float32)
        g_t = jnp.transpose(g4.astype(jnp.float32))
        dot = jnp.sum(att * g_t, axis=0, keepdims=True)
        for i in range(GRP):
            outb[s, 0, :, i * D : (i + 1) * D] = jnp.transpose(att[:, i * D : (i + 1) * D]).astype(jnp.bfloat16)
        acc[1, pl.ds(first, KEYS)] += jnp.dot(weights, g4, preferred_element_type=jnp.float32)
        dscore = (weights.astype(jnp.float32) * (nt(values, g4) - dot)).astype(jnp.bfloat16)
        dq = tn(keys, dscore) * SCALE
        for i in range(GRP):
            outb[s, 1, :, i * D : (i + 1) * D] = jnp.transpose(dq[:, i * D : (i + 1) * D]).astype(jnp.bfloat16)
        acc[0, pl.ds(first, KEYS)] += jnp.dot(dscore, q4, preferred_element_type=jnp.float32)
        for i, dst in enumerate((att_ref, dq_ref)):
            for cc in range(2):
                piece = outb.at[s, i, pl.ds(cc * TOK, TOK)]
                there = dst.at[:, pl.ds(col_q, BLK)]

                @pl.when(2 * s + cc == h)
                def _():
                    pltpu.make_async_copy(piece, there, out_recv.at[i]).start()

                @pl.when(2 * s + cc != h)
                def _():
                    pltpu.make_async_remote_copy(
                        src_ref=piece, dst_ref=there, send_sem=out_send.at[i], recv_sem=out_recv.at[i],
                        device_id=(c, 2 * s + cc), device_id_type=MESH,
                    ).start()

        return carry

    lax.fori_loop(0, 4, unit, 0)

    factors = (SCALE, 1.0)
    for i in range(2):
        hsend[1, i] = (acc[i, :BLK] * factors[i]).astype(jnp.bfloat16)
        pass_on(hsend.at[1, i], hrecv.at[1, i], part_send.at[1, i], part_recv.at[1, i], before)
    for i in range(2):
        arrived(hrecv.at[1, i], part_recv.at[1, i])
        hsend[0, i] = (acc[i, BLK : 2 * BLK] * factors[i] + hrecv[1, i].astype(jnp.float32)).astype(jnp.bfloat16)
        pass_on(hsend.at[0, i], hrecv.at[0, i], part_send.at[0, i], part_recv.at[0, i], before)
    for i, dst in enumerate((dk_ref, dv_ref)):
        arrived(hrecv.at[0, i], part_recv.at[0, i])
        mine = acc[i, 2 * BLK :] * factors[i]
        osend[i] = (mine + hrecv[0, i].astype(jnp.float32)).astype(jnp.bfloat16)
        there = dst.at[:, pl.ds(col_k, D)]
        pltpu.make_async_copy(
            osend.at[i, pl.ds(pl.multiple_of(h * TOK, TOK), TOK)], there, grad_recv.at[i]
        ).start()
        for dz, dk in peers:
            p = head_dev(dz, dk)
            pltpu.make_async_remote_copy(
                src_ref=osend.at[i, pl.ds(pl.multiple_of(p * TOK, TOK), TOK)], dst_ref=there,
                send_sem=grad_send.at[i], recv_sem=grad_recv.at[i], device_id=(c, p), device_id_type=MESH,
            ).start()

    for i, dst in enumerate((att_ref, dq_ref)):
        arrived(dst, out_recv.at[i])
    for i, dst in enumerate((dk_ref, dv_ref)):
        arrived(dst, grad_recv.at[i])
    sent = len(peers) * TOK
    for i in range(2):
        arrived(osend.at[i, pl.ds(0, sent)], grad_send.at[i])
        arrived(att_ref.at[:, pl.ds(0, len(peers) * BLK)], out_send.at[i])
        arrived(att_ref.at[:, pl.ds(0, len(peers) * BLK)], qg_send.at[i])
        arrived(docw.at[i], doc_send.at[i])
        for j in range(2):
            arrived(hsend.at[j, i], part_send.at[j, i])
            for r in range(2):
                arrived(chunk(i, r, 2 - j), halo_send.at[j, i, r])
    arrived(kv.at[:, pl.ds(0, sent)], kv_send)


def hand_over(*refs):
    sources, targets, stages, sems = refs[:4], refs[4:8], refs[8:12], refs[12]
    loads = [pltpu.make_async_copy(sources[i], stages[i], sems.at[0, i]) for i in range(4)]
    stores = [pltpu.make_async_copy(stages[i], targets[i], sems.at[1, i]) for i in range(4)]
    for load in loads:
        load.start()
    for load, store in zip(loads, stores):
        load.wait()
        store.start()
    for store in stores:
        store.wait()


def on_device(queries, stacked_keys, stacked_values, output_gradient, doc_ids):
    any_ref = pl.BlockSpec(memory_space=pl.ANY)
    dma = pltpu.SemaphoreType.DMA
    shapes = [jax.ShapeDtypeStruct(a.shape, a.dtype) for a in (queries, queries, stacked_keys, stacked_values)]
    results = pl.pallas_call(
        kernel,
        out_shape=shapes,
        in_specs=[any_ref] * 5,
        out_specs=[any_ref] * 4,
        scratch_shapes=[
            pltpu.VMEM((2, WIN, D), jnp.bfloat16),
            pltpu.VMEM((4, 2, SL, BLK), jnp.bfloat16),
            pltpu.VMEM((3, 1, BLK), jnp.int32),
            pltpu.VMEM((4, 8, SL), jnp.int32),
            pltpu.VMEM((4, 2, SL, BLK), jnp.bfloat16),
            pltpu.VMEM((2, WIN, D), jnp.float32),
            pltpu.VMEM((2, 2, BLK, D), jnp.bfloat16),
            pltpu.VMEM((2, 2, BLK, D), jnp.bfloat16),
            pltpu.VMEM((2, BLK, D), jnp.bfloat16),
            dma, dma((2,)), dma((2,)), dma((4,)), dma((2, 2, 2)), dma((2, 2, 2)), dma((2,)), dma((2,)), dma,
            dma((2,)), dma((2,)), dma((2, 2)), dma((2, 2)), dma((2,)), dma((2,)),
        ],
        compiler_params=pltpu.CompilerParams(
            collective_id=0, has_side_effects=True, vmem_limit_bytes=60 * 2**20
        ),
    )(queries, stacked_keys, stacked_values, output_gradient, doc_ids.reshape(1, -1))
    return pl.pallas_call(
        hand_over, out_shape=shapes, in_specs=[any_ref] * 4, out_specs=[any_ref] * 4,
        scratch_shapes=[pltpu.VMEM(a.shape, a.dtype) for a in shapes] + [dma((2, 4))],
        compiler_params=pltpu.CompilerParams(vmem_limit_bytes=60 * 2**20),
    )(*results)


def solution(mesh):
    tokens = P(("ctx", "head"), None)
    return jax.shard_map(
        on_device, mesh=mesh, in_specs=(tokens,) * 4 + (P("ctx"),), out_specs=(tokens,) * 4, check_vma=False
    )
```

```python
import math

import jax
import jax.numpy as jnp
from jax import lax
from jax.experimental import pallas as pl
from jax.experimental.pallas import tpu as pltpu
from jax.sharding import PartitionSpec as P

D = 128
TOK = 64
SL = 128
BLK = 512
HALF = 256
WIN = 1536
KEYS = 1152
GRP = 4
MESH = pl.DeviceIdType.MESH
SCALE = 1.0 / math.sqrt(D)
LOG2E = 1.4426950408889634


def nt(a, b):
    return lax.dot_general(a, b, (((1,), (1,)), ((), ())), preferred_element_type=jnp.float32)


def tn(a, b):
    return lax.dot_general(a, b, (((0,), (0,)), ((), ())), preferred_element_type=jnp.float32)


def kernel(
    q_ref, k_ref, v_ref, g_ref, doc_ref,
    att_ref, dq_ref, dk_ref, dv_ref,
    kv, qg, docw, startb, outb, acc, hsend, hrecv, osend, relay,
    kv_send, kv_recv, qg_send, qg_recv, halo_send, halo_recv, doc_send, doc_recv, own_sem,
    out_send, out_recv, part_send, part_recv, grad_send, grad_recv, extra_send, relay_send, relay_recv,
):
    n_ctx = lax.axis_size("ctx")
    c = lax.axis_index("ctx")
    h = lax.axis_index("head")
    zh = h // 2
    core = lax.rem(h, 2)

    def head_dev(dz, dk):
        return lax.rem(zh + dz, 4) * 2 + lax.rem(core + dk, 2)

    last, seam = n_ctx - 1, n_ctx // 2

    peers = [(0, 1), (1, 0), (1, 1), (3, 0), (3, 1), (2, 0), (2, 1)]

    own_row = pl.multiple_of(2 * BLK + h * TOK, TOK)
    col_q = pl.multiple_of(h * BLK, BLK)
    col_k = pl.multiple_of(h * D, D)
    tok_row = pl.multiple_of(core * TOK, TOK)
    for i, src in enumerate((k_ref, v_ref)):
        pltpu.make_async_copy(src.at[:, pl.ds(col_k, D)], kv.at[i, pl.ds(own_row, TOK)], kv_recv.at[i]).start()
    for i, src in enumerate((q_ref, g_ref)):
        pltpu.make_async_copy(
            src.at[:, pl.ds(col_q, BLK)], qg.at[zh, i, pl.ds(tok_row, TOK)], qg_recv.at[zh]
        ).start()
    pltpu.make_async_copy(doc_ref, docw.at[2], own_sem).start()

    @pl.when(c < 2)
    def _():
        kv[:, : 2 * BLK] = jnp.zeros((2, 2 * BLK, D), jnp.bfloat16)
        docw[0] = jnp.full((1, BLK), -1, jnp.int32)
        docw[1] = jnp.full((1, BLK), -1, jnp.int32)

    @pl.when((c == 0) | (c == seam) | (c == last))
    def _():
        hrecv[...] = jnp.zeros_like(hrecv)

    barrier = pltpu.get_barrier_semaphore()
    for dz, dk in peers:
        pl.semaphore_signal(barrier, inc=1, device_id=(c, head_dev(dz, dk)), device_id_type=MESH)
    has_before, has_after = c >= 1, c < last
    turning = ((c >= seam - 2) & (c <= seam)) | (c >= last - 1)
    near = [(has_before, c - 1), (has_after, c + 1)]
    for other in (seam - 2, seam - 1, seam, last - 1, last):
        near.append((turning & ((c < other - 1) | (c > other + 1)), other))
    partners = len(peers)
    for there, other in near:
        partners = partners + jnp.where(there, 1, 0)

        @pl.when(there)
        def _():
            pl.semaphore_signal(barrier, inc=1, device_id=(other, h), device_id_type=MESH)

    pl.semaphore_wait(barrier, partners)

    for i, src in enumerate((k_ref, v_ref)):
        for dz, dk in peers:
            p = head_dev(dz, dk)
            pltpu.make_async_remote_copy(
                src_ref=src.at[:, pl.ds(pl.multiple_of(p * D, D), D)],
                dst_ref=kv.at[i, pl.ds(own_row, TOK)],
                send_sem=kv_send, recv_sem=kv_recv.at[i], device_id=(c, p), device_id_type=MESH,
            ).start()

    after, before = (c + 1, h), (c - 1, h)

    def pass_on(src, dst, send_sem, recv_sem, to=after):
        pltpu.make_async_remote_copy(
            src_ref=src, dst_ref=dst, send_sem=send_sem, recv_sem=recv_sem, device_id=to, device_id_type=MESH
        ).start()

    def arrived(ref, sem):
        pltpu.make_async_copy(ref, ref, sem).wait()

    def chunk(i, r, block):
        return kv.at[i, pl.ds(block * BLK + r * HALF, HALF)]

    for dz, dk in peers[:5]:
        p = head_dev(dz, dk)
        for i, src in enumerate((q_ref, g_ref)):
            pltpu.make_async_remote_copy(
                src_ref=src.at[:, pl.ds(pl.multiple_of(p * BLK, BLK), BLK)],
                dst_ref=qg.at[zh, i, pl.ds(tok_row, TOK)],
                send_sem=qg_send.at[i], recv_sem=qg_recv.at[zh], device_id=(c, p), device_id_type=MESH,
            ).start()

    def way(r):
        return relay.at[0, pl.ds(r * HALF, HALF)]

    @pl.when(has_after)
    def _():
        pass_on(doc_ref, docw.at[1], doc_send.at[0], doc_recv.at[0])

    for i in range(2):
        arrived(kv.at[i, pl.ds(2 * BLK, BLK)], kv_recv.at[i])

        @pl.when(has_after & ((c != seam - 1) | (i == 1)))
        def _():
            for r in range(2):
                pass_on(chunk(i, r, 2), chunk(i, r, 1), halo_send.at[0, i, r], halo_recv.at[0, i, r])

        @pl.when((c == seam - 1) & (i == 0))
        def _():
            for r in range(2):
                pass_on(chunk(i, r, 2), way(r), halo_send.at[0, i, r], relay_recv.at[r], (last, h))

        @pl.when(c == seam - 2)
        def _():
            for r in range(2):
                if i == 0:
                    pass_on(chunk(i, r, 2), chunk(i, r, 0), extra_send.at[i, r], halo_recv.at[1, i, r], (seam, h))
                else:
                    pass_on(chunk(i, r, 2), way(r), extra_send.at[i, r], relay_recv.at[r], (last - 1, h))

    for dz, dk in peers[5:]:
        p = head_dev(dz, dk)
        for i, src in enumerate((q_ref, g_ref)):
            pltpu.make_async_remote_copy(
                src_ref=src.at[:, pl.ds(pl.multiple_of(p * BLK, BLK), BLK)],
                dst_ref=qg.at[zh, i, pl.ds(tok_row, TOK)],
                send_sem=qg_send.at[i], recv_sem=qg_recv.at[zh], device_id=(c, p), device_id_type=MESH,
            ).start()

    def turn(where, i, stage):
        @pl.when(c == where)
        def _():
            for r in range(2):
                arrived(way(r), relay_recv.at[r])
                pass_on(way(r), chunk(i, r, 1 - stage), relay_send.at[r], halo_recv.at[stage, i, r], (seam, h))

    turn(last, 0, 0)

    @pl.when(has_before)
    def _():
        arrived(docw.at[1], doc_recv.at[0])

        @pl.when(has_after)
        def _():
            pass_on(docw.at[1], docw.at[0], doc_send.at[1], doc_recv.at[1])

        for i in range(2):
            for r in range(2):
                arrived(chunk(i, r, 1), halo_recv.at[0, i, r])

                @pl.when(has_after & (c != seam - 1))
                def _():
                    pass_on(chunk(i, r, 1), chunk(i, r, 0), halo_send.at[1, i, r], halo_recv.at[1, i, r])

    turn(last - 1, 1, 1)
    acc[...] = jnp.zeros_like(acc)
    pltpu.make_async_copy(doc_ref, docw.at[2], own_sem).wait()

    @pl.when(c >= 2)
    def _():
        arrived(docw.at[0], doc_recv.at[1])

    docs = jnp.concatenate([docw[0], docw[1], docw[2]], axis=1)
    lane = lax.broadcasted_iota(jnp.int32, (1, WIN), 1)
    docs = jnp.where(lane + (c - 2) * BLK >= 0, docs, -1)
    docs = jnp.broadcast_to(docs, (8, WIN))
    lane = lax.broadcasted_iota(jnp.int32, (8, WIN), 1)
    begins = jnp.where((lane == 0) | (docs != pltpu.roll(docs, 1, 1)), lane, 0)
    step = 1
    while step < WIN:
        begins = jnp.maximum(begins, jnp.where(lane >= step, pltpu.roll(begins, step, 1), 0))
        step *= 2
    for s in range(4):
        startb[s] = begins[:, 2 * BLK + s * SL : 2 * BLK + (s + 1) * SL]

    @pl.when(c >= 2)
    def _():
        for i in range(2):
            for r in range(2):
                arrived(chunk(i, r, 0), halo_recv.at[1, i, r])

    def unit(j, carry):
        s = lax.rem(zh + jnp.where(j == 2, 3, jnp.where(j == 3, 2, j)), 4)
        pltpu.make_async_copy(qg.at[s], qg.at[s], qg_recv.at[s]).wait()
        first = pl.multiple_of(s * SL, SL)
        keys = kv[0, pl.ds(first, KEYS)]
        values = kv[1, pl.ds(first, KEYS)]
        q4 = jnp.concatenate([qg[s, 0, :, i * D : (i + 1) * D] for i in range(GRP)], axis=0)
        g4 = jnp.concatenate([qg[s, 1, :, i * D : (i + 1) * D] for i in range(GRP)], axis=0)
        start = startb[s][0:1]
        start = jnp.concatenate([start] * GRP, axis=1) - first
        scores = nt(keys, q4) * (SCALE * LOG2E)
        row = lax.broadcasted_iota(jnp.int32, (KEYS, GRP * SL), 0)
        column = lax.rem(lax.broadcasted_iota(jnp.int32, (1, GRP * SL), 1), SL) + 2 * BLK
        scores = jnp.where((row >= start) & (row <= column), scores, -jnp.inf)
        peak = jnp.max(scores, axis=0, keepdims=True)
        weights = jnp.exp2(scores - peak)
        total = jnp.sum(weights, axis=0, keepdims=True)
        weights = (weights * (1.0 / total)).astype(jnp.bfloat16)
        att = tn(values, weights).astype(jnp.bfloat16).astype(jnp.float32)
        g_t = jnp.transpose(g4.astype(jnp.float32))
        dot = jnp.sum(att * g_t, axis=0, keepdims=True)
        for i in range(GRP):
            outb[s, 0, :, i * D : (i + 1) * D] = jnp.transpose(att[:, i * D : (i + 1) * D]).astype(jnp.bfloat16)
        acc[1, pl.ds(first, KEYS)] += jnp.dot(weights, g4, preferred_element_type=jnp.float32)
        dscore = (weights.astype(jnp.float32) * (nt(values, g4) - dot)).astype(jnp.bfloat16)
        dq = tn(keys, dscore) * SCALE
        for i in range(GRP):
            outb[s, 1, :, i * D : (i + 1) * D] = jnp.transpose(dq[:, i * D : (i + 1) * D]).astype(jnp.bfloat16)
        acc[0, pl.ds(first, KEYS)] += jnp.dot(dscore, q4, preferred_element_type=jnp.float32)
        for i, dst in enumerate((att_ref, dq_ref)):
            for cc in range(2):
                piece = outb.at[s, i, pl.ds(cc * TOK, TOK)]
                there = dst.at[:, pl.ds(col_q, BLK)]

                @pl.when(2 * s + cc == h)
                def _():
                    pltpu.make_async_copy(piece, there, out_recv.at[i]).start()

                @pl.when(2 * s + cc != h)
                def _():
                    pltpu.make_async_remote_copy(
                        src_ref=piece, dst_ref=there, send_sem=out_send.at[i], recv_sem=out_recv.at[i],
                        device_id=(c, 2 * s + cc), device_id_type=MESH,
                    ).start()

        return carry

    lax.fori_loop(0, 4, unit, 0)

    factors = (SCALE, 1.0)

    def give(stage, i):
        here, there, sent = hsend.at[stage, i], hrecv.at[stage, i], part_send.at[stage, i]
        aside = -1

        side = (stage == 0) and (i == 0)

        @pl.when((c >= stage + 1) & (c != (seam if side else -1)))
        def _():
            pass_on(here, there, sent, part_recv.at[stage, i], before)

        if side:

            @pl.when(c == seam)
            def _():
                pass_on(here, relay.at[1], sent, relay_recv.at[2], (last, h))

    for i in range(2):
        hsend[1, i] = (acc[i, :BLK] * factors[i]).astype(jnp.bfloat16)
        give(1, i)
    for i in range(2):

        @pl.when(has_before & has_after)
        def _():
            arrived(hrecv.at[1, i], part_recv.at[1, i])

        hsend[0, i] = (acc[i, BLK : 2 * BLK] * factors[i] + hrecv[1, i].astype(jnp.float32)).astype(jnp.bfloat16)
        give(0, i)
    @pl.when(c == last)
    def _():
        arrived(relay.at[1], relay_recv.at[2])
        pass_on(relay.at[1], hrecv.at[0, 0], relay_send.at[2], part_recv.at[0, 0], (seam - 1, h))

    for i, dst in enumerate((dk_ref, dv_ref)):

        @pl.when(has_after)
        def _():
            arrived(hrecv.at[0, i], part_recv.at[0, i])

        mine = acc[i, 2 * BLK :] * factors[i]
        mine = mine + hrecv[0, i].astype(jnp.float32)

        osend[i] = mine.astype(jnp.bfloat16)
        there = dst.at[:, pl.ds(col_k, D)]
        pltpu.make_async_copy(
            osend.at[i, pl.ds(pl.multiple_of(h * TOK, TOK), TOK)], there, grad_recv.at[i]
        ).start()
        for dz, dk in peers:
            p = head_dev(dz, dk)
            pltpu.make_async_remote_copy(
                src_ref=osend.at[i, pl.ds(pl.multiple_of(p * TOK, TOK), TOK)], dst_ref=there,
                send_sem=grad_send.at[i], recv_sem=grad_recv.at[i], device_id=(c, p), device_id_type=MESH,
            ).start()

    for i, dst in enumerate((att_ref, dq_ref)):
        arrived(dst, out_recv.at[i])
    for i, dst in enumerate((dk_ref, dv_ref)):
        arrived(dst, grad_recv.at[i])
    sent = len(peers) * TOK
    for i in range(2):
        arrived(osend.at[i, pl.ds(0, sent)], grad_send.at[i])
        arrived(att_ref.at[:, pl.ds(0, len(peers) * BLK)], out_send.at[i])
        arrived(att_ref.at[:, pl.ds(0, len(peers) * BLK)], qg_send.at[i])
        for j in range(2):

            @pl.when(c >= j + 1)
            def _():
                arrived(hsend.at[j, i], part_send.at[j, i])

            @pl.when(has_after if j == 0 else has_before & has_after & (c != seam - 1))
            def _():
                for r in range(2):
                    arrived(chunk(i, r, 2 - j), halo_send.at[j, i, r])

        @pl.when(c == seam - 2)
        def _():
            for r in range(2):
                arrived(chunk(i, r, 2), extra_send.at[i, r])

    @pl.when(has_after)
    def _():
        arrived(docw.at[1], doc_send.at[0])

    @pl.when(has_before & has_after)
    def _():
        arrived(docw.at[1], doc_send.at[1])

    @pl.when(c == last)
    def _():
        arrived(relay.at[1], relay_send.at[2])

    @pl.when(c >= last - 1)
    def _():
        for r in range(2):
            arrived(way(r), relay_send.at[r])


    arrived(kv.at[:, pl.ds(0, sent)], kv_send)


def hand_over(*refs):
    sources, targets, stages, sems = refs[:4], refs[4:8], refs[8:12], refs[12]
    loads = [pltpu.make_async_copy(sources[i], stages[i], sems.at[0, i]) for i in range(4)]
    stores = [pltpu.make_async_copy(stages[i], targets[i], sems.at[1, i]) for i in range(4)]
    for load in loads:
        load.start()
    for load, store in zip(loads, stores):
        load.wait()
        store.start()
    for store in stores:
        store.wait()


def on_device(queries, stacked_keys, stacked_values, output_gradient, doc_ids):
    any_ref = pl.BlockSpec(memory_space=pl.ANY)
    dma = pltpu.SemaphoreType.DMA
    shapes = [jax.ShapeDtypeStruct(a.shape, a.dtype) for a in (queries, queries, stacked_keys, stacked_values)]
    results = pl.pallas_call(
        kernel,
        out_shape=shapes,
        in_specs=[any_ref] * 5,
        out_specs=[any_ref] * 4,
        scratch_shapes=[
            pltpu.VMEM((2, WIN, D), jnp.bfloat16),
            pltpu.VMEM((4, 2, SL, BLK), jnp.bfloat16),
            pltpu.VMEM((3, 1, BLK), jnp.int32),
            pltpu.VMEM((4, 8, SL), jnp.int32),
            pltpu.VMEM((4, 2, SL, BLK), jnp.bfloat16),
            pltpu.VMEM((2, WIN, D), jnp.float32),
            pltpu.VMEM((2, 2, BLK, D), jnp.bfloat16),
            pltpu.VMEM((2, 2, BLK, D), jnp.bfloat16),
            pltpu.VMEM((2, BLK, D), jnp.bfloat16),
            pltpu.VMEM((2, BLK, D), jnp.bfloat16),
            dma, dma((2,)), dma((2,)), dma((4,)), dma((2, 2, 2)), dma((2, 2, 2)), dma((2,)), dma((2,)), dma,
            dma((2,)), dma((2,)), dma((2, 2)), dma((2, 2)), dma((2,)), dma((2,)),
            dma((2, 2)), dma((3,)), dma((3,)),
        ],
        compiler_params=pltpu.CompilerParams(
            collective_id=0, has_side_effects=True, vmem_limit_bytes=60 * 2**20
        ),
    )(queries, stacked_keys, stacked_values, output_gradient, doc_ids.reshape(1, -1))
    return pl.pallas_call(
        hand_over, out_shape=shapes, in_specs=[any_ref] * 4, out_specs=[any_ref] * 4,
        scratch_shapes=[pltpu.VMEM(a.shape, a.dtype) for a in shapes] + [dma((2, 4))],
        compiler_params=pltpu.CompilerParams(vmem_limit_bytes=60 * 2**20),
    )(*results)


def solution(mesh):
    tokens = P(("ctx", "head"), None)
    return jax.shard_map(
        on_device, mesh=mesh, in_specs=(tokens,) * 4 + (P("ctx"),), out_specs=(tokens,) * 4, check_vma=False
    )
```

```python
import math

import jax
import jax.numpy as jnp
from jax import lax
from jax.experimental import pallas as pl
from jax.experimental.pallas import tpu as pltpu
from jax.sharding import PartitionSpec as P

D = 128
TOK = 64
SL = 128
BLK = 512
HALF = 256
WIN = 1536
KEYS = 1152
GRP = 4
MESH = pl.DeviceIdType.MESH
SCALE = 1.0 / math.sqrt(D)
LOG2E = 1.4426950408889634


def nt(a, b):
    return lax.dot_general(a, b, (((1,), (1,)), ((), ())), preferred_element_type=jnp.float32)


def tn(a, b):
    return lax.dot_general(a, b, (((0,), (0,)), ((), ())), preferred_element_type=jnp.float32)


def kernel(
    q_ref, k_ref, v_ref, g_ref, doc_ref,
    att_ref, dq_ref, dk_ref, dv_ref,
    kv, qg, docw, startb, outb, acc, hsend, hrecv, osend, relay, probs,
    kv_send, kv_recv, qg_send, qg_recv, halo_send, halo_recv, doc_send, doc_recv, own_sem,
    out_send, out_recv, part_send, part_recv, grad_send, grad_recv, extra_send, relay_send, relay_recv, go_sem,
):
    n_ctx = lax.axis_size("ctx")
    c = lax.axis_index("ctx")
    h = lax.axis_index("head")
    zh = h // 2
    core = lax.rem(h, 2)

    def head_dev(dz, dk):
        return lax.rem(zh + dz, 4) * 2 + lax.rem(core + dk, 2)

    last, seam = n_ctx - 1, n_ctx // 2

    peers = [(0, 1), (1, 0), (1, 1), (3, 0), (3, 1), (2, 0), (2, 1)]

    own_row = pl.multiple_of(2 * BLK + h * TOK, TOK)
    col_q = pl.multiple_of(h * BLK, BLK)
    col_k = pl.multiple_of(h * D, D)
    tok_row = pl.multiple_of(core * TOK, TOK)
    for i, src in enumerate((k_ref, v_ref)):
        pltpu.make_async_copy(src.at[:, pl.ds(col_k, D)], kv.at[i, pl.ds(own_row, TOK)], kv_recv.at[i]).start()
    for i, src in enumerate((q_ref, g_ref)):
        pltpu.make_async_copy(
            src.at[:, pl.ds(col_q, BLK)], qg.at[zh, i, pl.ds(tok_row, TOK)], qg_recv.at[zh]
        ).start()
    pltpu.make_async_copy(doc_ref, docw.at[2], own_sem).start()

    @pl.when(c < 2)
    def _():
        kv[:, : 2 * BLK] = jnp.zeros((2, 2 * BLK, D), jnp.bfloat16)
        docw[0] = jnp.full((1, BLK), -1, jnp.int32)
        docw[1] = jnp.full((1, BLK), -1, jnp.int32)

    @pl.when((c == 0) | (c == seam - 1) | (c == last))
    def _():
        hrecv[...] = jnp.zeros_like(hrecv)

    barrier = pltpu.get_barrier_semaphore()
    for dz, dk in peers:
        pl.semaphore_signal(barrier, inc=1, device_id=(c, head_dev(dz, dk)), device_id_type=MESH)
    has_before, has_after = c >= 1, c < last
    turning = ((c >= seam - 2) & (c <= seam)) | (c >= last - 1)
    near = [(has_before, c - 1), (has_after, c + 1)]
    for other in (seam - 2, seam - 1, seam, last - 1, last):
        near.append((turning & ((c < other - 1) | (c > other + 1)), other))
    partners = len(peers)
    for there, other in near:
        partners = partners + jnp.where(there, 1, 0)

        @pl.when(there)
        def _():
            pl.semaphore_signal(barrier, inc=1, device_id=(other, h), device_id_type=MESH)

    pl.semaphore_wait(barrier, partners)

    for i, src in enumerate((k_ref, v_ref)):
        for dz, dk in peers:
            p = head_dev(dz, dk)
            pltpu.make_async_remote_copy(
                src_ref=src.at[:, pl.ds(pl.multiple_of(p * D, D), D)],
                dst_ref=kv.at[i, pl.ds(own_row, TOK)],
                send_sem=kv_send, recv_sem=kv_recv.at[i], device_id=(c, p), device_id_type=MESH,
            ).start()

    after, before = (c + 1, h), (c - 1, h)

    def pass_on(src, dst, send_sem, recv_sem, to=after):
        pltpu.make_async_remote_copy(
            src_ref=src, dst_ref=dst, send_sem=send_sem, recv_sem=recv_sem, device_id=to, device_id_type=MESH
        ).start()

    def arrived(ref, sem):
        pltpu.make_async_copy(ref, ref, sem).wait()

    def chunk(i, r, block):
        return kv.at[i, pl.ds(block * BLK + r * HALF, HALF)]

    for dz, dk in peers[:5]:
        p = head_dev(dz, dk)
        for i, src in enumerate((q_ref, g_ref)):
            pltpu.make_async_remote_copy(
                src_ref=src.at[:, pl.ds(pl.multiple_of(p * BLK, BLK), BLK)],
                dst_ref=qg.at[zh, i, pl.ds(tok_row, TOK)],
                send_sem=qg_send.at[i], recv_sem=qg_recv.at[zh], device_id=(c, p), device_id_type=MESH,
            ).start()

    def way(r):
        return relay.at[0, pl.ds(r * HALF, HALF)]

    @pl.when(has_after)
    def _():
        pass_on(doc_ref, docw.at[1], doc_send.at[0], doc_recv.at[0])

    for i in range(2):
        arrived(kv.at[i, pl.ds(2 * BLK, BLK)], kv_recv.at[i])

        @pl.when(has_after & ((c != seam - 1) | (i == 1)))
        def _():
            for r in range(2):
                pass_on(chunk(i, r, 2), chunk(i, r, 1), halo_send.at[0, i, r], halo_recv.at[0, i, r])

        @pl.when((c == seam - 1) & (i == 0))
        def _():
            for r in range(2):
                pass_on(chunk(i, r, 2), way(r), halo_send.at[0, i, r], relay_recv.at[r], (last, h))

        @pl.when(c == seam - 2)
        def _():
            for r in range(2):
                if i == 0:
                    pass_on(chunk(i, r, 2), chunk(i, r, 0), extra_send.at[i, r], halo_recv.at[1, i, r], (seam, h))
                else:
                    pass_on(chunk(i, r, 2), way(r), extra_send.at[i, r], relay_recv.at[r], (last - 1, h))

    for dz, dk in peers[5:]:
        p = head_dev(dz, dk)
        for i, src in enumerate((q_ref, g_ref)):
            pltpu.make_async_remote_copy(
                src_ref=src.at[:, pl.ds(pl.multiple_of(p * BLK, BLK), BLK)],
                dst_ref=qg.at[zh, i, pl.ds(tok_row, TOK)],
                send_sem=qg_send.at[i], recv_sem=qg_recv.at[zh], device_id=(c, p), device_id_type=MESH,
            ).start()

    def turn(where, i, stage):
        @pl.when(c == where)
        def _():
            for r in range(2):
                arrived(way(r), relay_recv.at[r])
                pass_on(way(r), chunk(i, r, 1 - stage), relay_send.at[r], halo_recv.at[stage, i, r], (seam, h))

    turn(last, 0, 0)

    @pl.when(has_before)
    def _():
        arrived(docw.at[1], doc_recv.at[0])

        @pl.when(has_after)
        def _():
            pass_on(docw.at[1], docw.at[0], doc_send.at[1], doc_recv.at[1])

        for i in range(2):
            for r in range(2):
                arrived(chunk(i, r, 1), halo_recv.at[0, i, r])

                @pl.when(has_after & (c != seam - 1))
                def _():
                    pass_on(chunk(i, r, 1), chunk(i, r, 0), halo_send.at[1, i, r], halo_recv.at[1, i, r])

    turn(last - 1, 1, 1)
    acc[...] = jnp.zeros_like(acc)
    pltpu.make_async_copy(doc_ref, docw.at[2], own_sem).wait()

    @pl.when(c >= 2)
    def _():
        arrived(docw.at[0], doc_recv.at[1])

    docs = jnp.concatenate([docw[0], docw[1], docw[2]], axis=1)
    lane = lax.broadcasted_iota(jnp.int32, (1, WIN), 1)
    docs = jnp.where(lane + (c - 2) * BLK >= 0, docs, -1)
    docs = jnp.broadcast_to(docs, (8, WIN))
    lane = lax.broadcasted_iota(jnp.int32, (8, WIN), 1)
    begins = jnp.where((lane == 0) | (docs != pltpu.roll(docs, 1, 1)), lane, 0)
    step = 1
    while step < WIN:
        begins = jnp.maximum(begins, jnp.where(lane >= step, pltpu.roll(begins, step, 1), 0))
        step *= 2
    for s in range(4):
        startb[s] = begins[:, 2 * BLK + s * SL : 2 * BLK + (s + 1) * SL]

    def earliest(i):
        @pl.when(c >= 2)
        def _():
            for r in range(2):
                arrived(chunk(i, r, 0), halo_recv.at[1, i, r])

    def stacked(s, which):
        return jnp.concatenate([qg[s, which, :, i * D : (i + 1) * D] for i in range(GRP)], axis=0)

    def weigh(s):
        arrived(qg.at[s], qg_recv.at[s])
        first = pl.multiple_of(s * SL, SL)
        q4 = stacked(s, 0)
        start = startb[s][0:1]
        start = jnp.concatenate([start] * GRP, axis=1) - first
        early, late = 2 * BLK, SL
        row = lax.broadcasted_iota(jnp.int32, (early, GRP * SL), 0)
        far = nt(kv[0, pl.ds(first, early)], q4) * (SCALE * LOG2E)
        far = jnp.where(row >= start, far, -jnp.inf)
        row = lax.broadcasted_iota(jnp.int32, (late, GRP * SL), 0)
        column = lax.rem(lax.broadcasted_iota(jnp.int32, (1, GRP * SL), 1), SL)
        close = nt(kv[0, pl.ds(pl.multiple_of(first + early, SL), late)], q4) * (SCALE * LOG2E)
        close = jnp.where((row >= start - early) & (row <= column), close, -jnp.inf)
        peak = jnp.maximum(jnp.max(far, axis=0, keepdims=True), jnp.max(close, axis=0, keepdims=True))
        far, close = jnp.exp2(far - peak), jnp.exp2(close - peak)
        part = 1.0 / (jnp.sum(far, axis=0, keepdims=True) + jnp.sum(close, axis=0, keepdims=True))
        probs[s, :early] = (far * part).astype(jnp.bfloat16)
        probs[s, early:] = (close * part).astype(jnp.bfloat16)

    def send_back(s, i):
        dst = (att_ref, dq_ref)[i]
        for cc in range(2):
            piece = outb.at[s, i, pl.ds(cc * TOK, TOK)]
            there = dst.at[:, pl.ds(col_q, BLK)]

            @pl.when(2 * s + cc == h)
            def _():
                pltpu.make_async_copy(piece, there, out_recv.at[i]).start()

            @pl.when(2 * s + cc != h)
            def _():
                pltpu.make_async_remote_copy(
                    src_ref=piece, dst_ref=there, send_sem=out_send.at[i], recv_sem=out_recv.at[i],
                    device_id=(c, 2 * s + cc), device_id_type=MESH,
                ).start()

    def weigh_near(j, carry):
        weigh(lax.rem(zh + jnp.where(j == 2, 3, j), 4))
        return carry

    def unit(j, carry):
        s = lax.rem(zh + jnp.where(j == 0, 1, jnp.where(j == 1, 3, jnp.where(j == 2, 0, 2))), 4)

        @pl.when(j == 3)
        def _():
            weigh(s)

        first = pl.multiple_of(s * SL, SL)
        values = kv[1, pl.ds(first, KEYS)]
        weights = probs[s]
        g4 = stacked(s, 1)
        att = tn(values, weights).astype(jnp.bfloat16).astype(jnp.float32)
        for i in range(GRP):
            outb[s, 0, :, i * D : (i + 1) * D] = jnp.transpose(att[:, i * D : (i + 1) * D]).astype(jnp.bfloat16)
        send_back(s, 0)
        dot = jnp.sum(att * jnp.transpose(g4.astype(jnp.float32)), axis=0, keepdims=True)
        dscore = (weights.astype(jnp.float32) * (nt(values, g4) - dot)).astype(jnp.bfloat16)
        dq = tn(kv[0, pl.ds(first, KEYS)], dscore) * SCALE
        for i in range(GRP):
            outb[s, 1, :, i * D : (i + 1) * D] = jnp.transpose(dq[:, i * D : (i + 1) * D]).astype(jnp.bfloat16)
        send_back(s, 1)
        acc[0, pl.ds(first, KEYS)] += jnp.dot(dscore, stacked(s, 0), preferred_element_type=jnp.float32)
        acc[1, pl.ds(first, KEYS)] += jnp.dot(weights, g4, preferred_element_type=jnp.float32)
        return carry

    earliest(0)
    lax.fori_loop(0, 3, weigh_near, 0)
    earliest(1)

    @pl.when(c == 1)
    def _():
        pl.semaphore_signal(go_sem, inc=1, device_id=(0, h), device_id_type=MESH)

    @pl.when(c == 0)
    def _():
        pl.semaphore_wait(go_sem, 1)

    lax.fori_loop(0, 4, unit, 0)

    factors = (SCALE, 1.0)

    def give(stage, i):
        here, sent = hsend.at[stage, i], part_send.at[stage, i]

        @pl.when((c >= stage + 1) & (c != (seam if stage == 1 else -1)))
        def _():
            pass_on(here, hrecv.at[stage, i], sent, part_recv.at[stage, i], before)

        if stage == 1:

            @pl.when(c == seam)
            def _():
                pass_on(here, relay.at[i], sent, relay_recv.at[i], (seam - 2, h))

    for i in range(2):
        hsend[1, i] = (acc[i, :BLK] * factors[i]).astype(jnp.bfloat16)
        give(1, i)
    for i in range(2):

        @pl.when(has_before & has_after & (c != seam - 1))
        def _():
            arrived(hrecv.at[1, i], part_recv.at[1, i])

        hsend[0, i] = (acc[i, BLK : 2 * BLK] * factors[i] + hrecv[1, i].astype(jnp.float32)).astype(jnp.bfloat16)
        give(0, i)
    for i, dst in enumerate((dk_ref, dv_ref)):

        @pl.when(has_after)
        def _():
            arrived(hrecv.at[0, i], part_recv.at[0, i])

        mine = acc[i, 2 * BLK :] * factors[i]
        mine = mine + hrecv[0, i].astype(jnp.float32)


        @pl.when(c != seam - 2)
        def _():
            osend[i] = mine.astype(jnp.bfloat16)

        @pl.when(c == seam - 2)
        def _():
            arrived(relay.at[i], relay_recv.at[i])
            osend[i] = (mine + relay[i].astype(jnp.float32)).astype(jnp.bfloat16)

        there = dst.at[:, pl.ds(col_k, D)]
        pltpu.make_async_copy(
            osend.at[i, pl.ds(pl.multiple_of(h * TOK, TOK), TOK)], there, grad_recv.at[i]
        ).start()
        for dz, dk in peers:
            p = head_dev(dz, dk)
            pltpu.make_async_remote_copy(
                src_ref=osend.at[i, pl.ds(pl.multiple_of(p * TOK, TOK), TOK)], dst_ref=there,
                send_sem=grad_send.at[i], recv_sem=grad_recv.at[i], device_id=(c, p), device_id_type=MESH,
            ).start()

    for i, dst in enumerate((att_ref, dq_ref)):
        arrived(dst, out_recv.at[i])
    for i, dst in enumerate((dk_ref, dv_ref)):
        arrived(dst, grad_recv.at[i])
    sent = len(peers) * TOK
    for i in range(2):
        arrived(osend.at[i, pl.ds(0, sent)], grad_send.at[i])
        arrived(att_ref.at[:, pl.ds(0, len(peers) * BLK)], out_send.at[i])
        arrived(att_ref.at[:, pl.ds(0, len(peers) * BLK)], qg_send.at[i])
        for j in range(2):

            @pl.when(c >= j + 1)
            def _():
                arrived(hsend.at[j, i], part_send.at[j, i])

            @pl.when(has_after if j == 0 else has_before & has_after & (c != seam - 1))
            def _():
                for r in range(2):
                    arrived(chunk(i, r, 2 - j), halo_send.at[j, i, r])

        @pl.when(c == seam - 2)
        def _():
            for r in range(2):
                arrived(chunk(i, r, 2), extra_send.at[i, r])

    @pl.when(has_after)
    def _():
        arrived(docw.at[1], doc_send.at[0])

    @pl.when(has_before & has_after)
    def _():
        arrived(docw.at[1], doc_send.at[1])

    @pl.when(c >= last - 1)
    def _():
        for r in range(2):
            arrived(way(r), relay_send.at[r])


    arrived(kv.at[:, pl.ds(0, sent)], kv_send)


def hand_over(*refs):
    sources, targets, stages, sems = refs[:4], refs[4:8], refs[8:12], refs[12]
    loads = [pltpu.make_async_copy(sources[i], stages[i], sems.at[0, i]) for i in range(4)]
    stores = [pltpu.make_async_copy(stages[i], targets[i], sems.at[1, i]) for i in range(4)]
    for load in loads:
        load.start()
    for load, store in zip(loads, stores):
        load.wait()
        store.start()
    for store in stores:
        store.wait()


def on_device(queries, stacked_keys, stacked_values, output_gradient, doc_ids):
    any_ref = pl.BlockSpec(memory_space=pl.ANY)
    dma = pltpu.SemaphoreType.DMA
    shapes = [jax.ShapeDtypeStruct(a.shape, a.dtype) for a in (queries, queries, stacked_keys, stacked_values)]
    results = pl.pallas_call(
        kernel,
        out_shape=shapes,
        in_specs=[any_ref] * 5,
        out_specs=[any_ref] * 4,
        scratch_shapes=[
            pltpu.VMEM((2, WIN, D), jnp.bfloat16),
            pltpu.VMEM((4, 2, SL, BLK), jnp.bfloat16),
            pltpu.VMEM((3, 1, BLK), jnp.int32),
            pltpu.VMEM((4, 8, SL), jnp.int32),
            pltpu.VMEM((4, 2, SL, BLK), jnp.bfloat16),
            pltpu.VMEM((2, WIN, D), jnp.float32),
            pltpu.VMEM((2, 2, BLK, D), jnp.bfloat16),
            pltpu.VMEM((2, 2, BLK, D), jnp.bfloat16),
            pltpu.VMEM((2, BLK, D), jnp.bfloat16),
            pltpu.VMEM((2, BLK, D), jnp.bfloat16),
            pltpu.VMEM((4, KEYS, GRP * SL), jnp.bfloat16),
            dma, dma((2,)), dma((2,)), dma((4,)), dma((2, 2, 2)), dma((2, 2, 2)), dma((2,)), dma((2,)), dma,
            dma((2,)), dma((2,)), dma((2, 2)), dma((2, 2)), dma((2,)), dma((2,)),
            dma((2, 2)), dma((3,)), dma((3,)), pltpu.SemaphoreType.REGULAR,
        ],
        compiler_params=pltpu.CompilerParams(
            collective_id=0, has_side_effects=True, vmem_limit_bytes=60 * 2**20
        ),
    )(queries, stacked_keys, stacked_values, output_gradient, doc_ids.reshape(1, -1))
    return pl.pallas_call(
        hand_over, out_shape=shapes, in_specs=[any_ref] * 4, out_specs=[any_ref] * 4,
        scratch_shapes=[pltpu.VMEM(a.shape, a.dtype) for a in shapes] + [dma((2, 4))],
        compiler_params=pltpu.CompilerParams(vmem_limit_bytes=60 * 2**20),
    )(*results)


def solution(mesh):
    tokens = P(("ctx", "head"), None)
    return jax.shard_map(
        on_device, mesh=mesh, in_specs=(tokens,) * 4 + (P("ctx"),), out_specs=(tokens,) * 4, check_vma=False
    )
```

```python
import math

import jax
import jax.numpy as jnp
from jax import lax
from jax.experimental import pallas as pl
from jax.experimental.pallas import tpu as pltpu
from jax.sharding import PartitionSpec as P

D = 128
TOK = 64
SL = 128
BLK = 512
HALF = 256
WIN = 1536
KEYS = 1152
GRP = 4
MESH = pl.DeviceIdType.MESH
SCALE = 1.0 / math.sqrt(D)
LOG2E = 1.4426950408889634


def nt(a, b):
    return lax.dot_general(a, b, (((1,), (1,)), ((), ())), preferred_element_type=jnp.float32)


def tn(a, b):
    return lax.dot_general(a, b, (((0,), (0,)), ((), ())), preferred_element_type=jnp.float32)


def kernel(
    q_ref, k_ref, v_ref, g_ref, doc_ref,
    att_ref, dq_ref, dk_ref, dv_ref,
    kv, qg, docw, startb, outb, acc, hsend, hrecv, osend, relay, probs,
    kv_send, kv_recv, qg_send, qg_recv, halo_send, halo_recv, doc_send, doc_recv, own_sem,
    out_send, out_recv, part_send, part_recv, grad_send, grad_recv, extra_send, relay_send, relay_recv, go_sem,
):
    n_ctx = lax.axis_size("ctx")
    c = lax.axis_index("ctx")
    h = lax.axis_index("head")
    zh = h // 2
    core = lax.rem(h, 2)

    def head_dev(dz, dk):
        return lax.rem(zh + dz, 4) * 2 + lax.rem(core + dk, 2)

    last, seam = n_ctx - 1, n_ctx // 2

    peers = [(0, 1), (1, 0), (1, 1), (3, 0), (3, 1), (2, 0), (2, 1)]

    own_row = pl.multiple_of(2 * BLK + h * TOK, TOK)
    col_q = pl.multiple_of(h * BLK, BLK)
    col_k = pl.multiple_of(h * D, D)
    tok_row = pl.multiple_of(core * TOK, TOK)
    for i, src in enumerate((k_ref, v_ref)):
        pltpu.make_async_copy(src.at[:, pl.ds(col_k, D)], kv.at[i, pl.ds(own_row, TOK)], kv_recv.at[i]).start()
    for i, src in enumerate((q_ref, g_ref)):
        pltpu.make_async_copy(
            src.at[:, pl.ds(col_q, BLK)], qg.at[zh, i, pl.ds(tok_row, TOK)], qg_recv.at[zh]
        ).start()
    pltpu.make_async_copy(doc_ref, docw.at[2], own_sem).start()

    @pl.when(c < 2)
    def _():
        kv[:, : 2 * BLK] = jnp.zeros((2, 2 * BLK, D), jnp.bfloat16)
        docw[0] = jnp.full((1, BLK), -1, jnp.int32)
        docw[1] = jnp.full((1, BLK), -1, jnp.int32)

    @pl.when((c == 0) | (c == seam - 1) | (c == last))
    def _():
        hrecv[...] = jnp.zeros_like(hrecv)

    barrier = pltpu.get_barrier_semaphore()
    for dz, dk in peers:
        pl.semaphore_signal(barrier, inc=1, device_id=(c, head_dev(dz, dk)), device_id_type=MESH)
    has_before, has_after = c >= 1, c < last
    turning = ((c >= seam - 2) & (c <= seam)) | (c >= last - 1)
    near = [(has_before, c - 1), (has_after, c + 1)]
    for other in (seam - 2, seam - 1, seam, last - 1, last):
        near.append((turning & ((c < other - 1) | (c > other + 1)), other))
    partners = len(peers)
    for there, other in near:
        partners = partners + jnp.where(there, 1, 0)

        @pl.when(there)
        def _():
            pl.semaphore_signal(barrier, inc=1, device_id=(other, h), device_id_type=MESH)

    pl.semaphore_wait(barrier, partners)

    for i, src in enumerate((k_ref, v_ref)):
        for dz, dk in peers:
            p = head_dev(dz, dk)
            pltpu.make_async_remote_copy(
                src_ref=src.at[:, pl.ds(pl.multiple_of(p * D, D), D)],
                dst_ref=kv.at[i, pl.ds(own_row, TOK)],
                send_sem=kv_send, recv_sem=kv_recv.at[i], device_id=(c, p), device_id_type=MESH,
            ).start()

    after, before = (c + 1, h), (c - 1, h)

    def pass_on(src, dst, send_sem, recv_sem, to=after):
        pltpu.make_async_remote_copy(
            src_ref=src, dst_ref=dst, send_sem=send_sem, recv_sem=recv_sem, device_id=to, device_id_type=MESH
        ).start()

    def arrived(ref, sem):
        pltpu.make_async_copy(ref, ref, sem).wait()

    def chunk(i, r, block):
        return kv.at[i, pl.ds(block * BLK + r * HALF, HALF)]

    for dz, dk in peers[:5]:
        p = head_dev(dz, dk)
        for i, src in enumerate((q_ref, g_ref)):
            pltpu.make_async_remote_copy(
                src_ref=src.at[:, pl.ds(pl.multiple_of(p * BLK, BLK), BLK)],
                dst_ref=qg.at[zh, i, pl.ds(tok_row, TOK)],
                send_sem=qg_send.at[i], recv_sem=qg_recv.at[zh], device_id=(c, p), device_id_type=MESH,
            ).start()

    def way(r):
        return relay.at[0, pl.ds(r * HALF, HALF)]

    @pl.when(has_after)
    def _():
        pass_on(doc_ref, docw.at[1], doc_send.at[0], doc_recv.at[0])

    for i in range(2):
        arrived(kv.at[i, pl.ds(2 * BLK, BLK)], kv_recv.at[i])

        @pl.when(has_after & ((c != seam - 1) | (i == 1)))
        def _():
            for r in range(2):
                pass_on(chunk(i, r, 2), chunk(i, r, 1), halo_send.at[0, i, r], halo_recv.at[0, i, r])

        @pl.when((c == seam - 1) & (i == 0))
        def _():
            for r in range(2):
                pass_on(chunk(i, r, 2), way(r), halo_send.at[0, i, r], relay_recv.at[r], (last, h))

        @pl.when(c == seam - 2)
        def _():
            for r in range(2):
                if i == 0:
                    pass_on(chunk(i, r, 2), chunk(i, r, 0), extra_send.at[i, r], halo_recv.at[1, i, r], (seam, h))
                else:
                    pass_on(chunk(i, r, 2), way(r), extra_send.at[i, r], relay_recv.at[r], (last - 1, h))

    for dz, dk in peers[5:]:
        p = head_dev(dz, dk)
        for i, src in enumerate((q_ref, g_ref)):
            pltpu.make_async_remote_copy(
                src_ref=src.at[:, pl.ds(pl.multiple_of(p * BLK, BLK), BLK)],
                dst_ref=qg.at[zh, i, pl.ds(tok_row, TOK)],
                send_sem=qg_send.at[i], recv_sem=qg_recv.at[zh], device_id=(c, p), device_id_type=MESH,
            ).start()

    def turn(where, i, stage):
        @pl.when(c == where)
        def _():
            for r in range(2):
                arrived(way(r), relay_recv.at[r])
                pass_on(way(r), chunk(i, r, 1 - stage), relay_send.at[r], halo_recv.at[stage, i, r], (seam, h))

    turn(last, 0, 0)

    @pl.when(has_before)
    def _():
        arrived(docw.at[1], doc_recv.at[0])

        @pl.when(has_after)
        def _():
            pass_on(docw.at[1], docw.at[0], doc_send.at[1], doc_recv.at[1])

        for i in range(2):
            for r in range(2):
                arrived(chunk(i, r, 1), halo_recv.at[0, i, r])

                @pl.when(has_after & (c != seam - 1))
                def _():
                    pass_on(chunk(i, r, 1), chunk(i, r, 0), halo_send.at[1, i, r], halo_recv.at[1, i, r])

    turn(last - 1, 1, 1)
    acc[...] = jnp.zeros_like(acc)
    pltpu.make_async_copy(doc_ref, docw.at[2], own_sem).wait()

    @pl.when(c >= 2)
    def _():
        arrived(docw.at[0], doc_recv.at[1])

    docs = jnp.concatenate([docw[0], docw[1], docw[2]], axis=1)
    lane = lax.broadcasted_iota(jnp.int32, (1, WIN), 1)
    docs = jnp.where(lane + (c - 2) * BLK >= 0, docs, -1)
    docs = jnp.broadcast_to(docs, (8, WIN))
    lane = lax.broadcasted_iota(jnp.int32, (8, WIN), 1)
    begins = jnp.where((lane == 0) | (docs != pltpu.roll(docs, 1, 1)), lane, 0)
    step = 1
    while step < WIN:
        begins = jnp.maximum(begins, jnp.where(lane >= step, pltpu.roll(begins, step, 1), 0))
        step *= 2
    for s in range(4):
        startb[s] = begins[:, 2 * BLK + s * SL : 2 * BLK + (s + 1) * SL]

    def earliest(i):
        @pl.when(c >= 2)
        def _():
            for r in range(2):
                arrived(chunk(i, r, 0), halo_recv.at[1, i, r])

    def stacked(s, which):
        return jnp.concatenate([qg[s, which, :, i * D : (i + 1) * D] for i in range(GRP)], axis=0)

    def weigh(s):
        arrived(qg.at[s], qg_recv.at[s])
        first = pl.multiple_of(s * SL, SL)
        q4 = stacked(s, 0)
        start = startb[s][0:1]
        start = jnp.concatenate([start] * GRP, axis=1) - first
        early, late = 2 * BLK, SL
        row = lax.broadcasted_iota(jnp.int32, (early, GRP * SL), 0)
        far = nt(kv[0, pl.ds(first, early)], q4) * (SCALE * LOG2E)
        far = jnp.where(row >= start, far, -jnp.inf)
        row = lax.broadcasted_iota(jnp.int32, (late, GRP * SL), 0)
        column = lax.rem(lax.broadcasted_iota(jnp.int32, (1, GRP * SL), 1), SL)
        close = nt(kv[0, pl.ds(pl.multiple_of(first + early, SL), late)], q4) * (SCALE * LOG2E)
        close = jnp.where((row >= start - early) & (row <= column), close, -jnp.inf)
        peak = jnp.maximum(jnp.max(far, axis=0, keepdims=True), jnp.max(close, axis=0, keepdims=True))
        far, close = jnp.exp2(far - peak), jnp.exp2(close - peak)
        part = 1.0 / (jnp.sum(far, axis=0, keepdims=True) + jnp.sum(close, axis=0, keepdims=True))
        probs[s, :early] = (far * part).astype(jnp.bfloat16)
        probs[s, early:] = (close * part).astype(jnp.bfloat16)

    def send_back(s, i):
        dst = (att_ref, dq_ref)[i]
        for cc in range(2):
            piece = outb.at[s, i, pl.ds(cc * TOK, TOK)]
            there = dst.at[:, pl.ds(col_q, BLK)]

            @pl.when(2 * s + cc == h)
            def _():
                pltpu.make_async_copy(piece, there, out_recv.at[i]).start()

            @pl.when(2 * s + cc != h)
            def _():
                pltpu.make_async_remote_copy(
                    src_ref=piece, dst_ref=there, send_sem=out_send.at[i], recv_sem=out_recv.at[i],
                    device_id=(c, 2 * s + cc), device_id_type=MESH,
                ).start()

    def weigh_near(j, carry):
        weigh(lax.rem(zh + jnp.where(j == 2, 3, j), 4))
        return carry

    def unit(j, carry):
        s = lax.rem(zh + jnp.where(j == 0, 1, jnp.where(j == 1, 3, jnp.where(j == 2, 0, 2))), 4)

        @pl.when(j == 3)
        def _():
            weigh(s)

        first = pl.multiple_of(s * SL, SL)
        values = kv[1, pl.ds(first, KEYS)]
        weights = probs[s]
        g4 = stacked(s, 1)
        att = tn(values, weights).astype(jnp.bfloat16).astype(jnp.float32)
        for i in range(GRP):
            outb[s, 0, :, i * D : (i + 1) * D] = jnp.transpose(att[:, i * D : (i + 1) * D]).astype(jnp.bfloat16)
        send_back(s, 0)
        dot = jnp.sum(att * jnp.transpose(g4.astype(jnp.float32)), axis=0, keepdims=True)
        dscore = (weights.astype(jnp.float32) * (nt(values, g4) - dot)).astype(jnp.bfloat16)
        dq = tn(kv[0, pl.ds(first, KEYS)], dscore) * SCALE
        for i in range(GRP):
            outb[s, 1, :, i * D : (i + 1) * D] = jnp.transpose(dq[:, i * D : (i + 1) * D]).astype(jnp.bfloat16)
        send_back(s, 1)
        acc[0, pl.ds(first, KEYS)] += jnp.dot(dscore, stacked(s, 0), preferred_element_type=jnp.float32)
        acc[1, pl.ds(first, KEYS)] += jnp.dot(weights, g4, preferred_element_type=jnp.float32)
        return carry

    earliest(0)
    lax.fori_loop(0, 3, weigh_near, 0)
    earliest(1)

    @pl.when(c == 1)
    def _():
        pl.semaphore_signal(go_sem, inc=1, device_id=(0, h), device_id_type=MESH)

    @pl.when(c == 0)
    def _():
        pl.semaphore_wait(go_sem, 1)

    lax.fori_loop(0, 4, unit, 0)

    factors = (SCALE, 1.0)

    def give(stage, i):
        here, sent = hsend.at[stage, i], part_send.at[stage, i]

        @pl.when((c >= stage + 1) & (c != (seam if stage == 1 else -1)))
        def _():
            pass_on(here, hrecv.at[stage, i], sent, part_recv.at[stage, i], before)

        if stage == 1:

            @pl.when(c == seam)
            def _():
                pass_on(here, relay.at[i], sent, relay_recv.at[i], (seam - 2, h))

    for i in range(2):
        hsend[1, i] = (acc[i, :BLK] * factors[i]).astype(jnp.bfloat16)
        give(1, i)
    for i in range(2):

        @pl.when(has_before & has_after & (c != seam - 1))
        def _():
            arrived(hrecv.at[1, i], part_recv.at[1, i])

        hsend[0, i] = (acc[i, BLK : 2 * BLK] * factors[i] + hrecv[1, i].astype(jnp.float32)).astype(jnp.bfloat16)
        give(0, i)
    for i, dst in enumerate((dk_ref, dv_ref)):

        @pl.when(has_after)
        def _():
            arrived(hrecv.at[0, i], part_recv.at[0, i])

        mine = acc[i, 2 * BLK :] * factors[i]
        mine = mine + hrecv[0, i].astype(jnp.float32)


        @pl.when(c != seam - 2)
        def _():
            osend[i] = mine.astype(jnp.bfloat16)

        @pl.when(c == seam - 2)
        def _():
            arrived(relay.at[i], relay_recv.at[i])
            osend[i] = (mine + relay[i].astype(jnp.float32)).astype(jnp.bfloat16)

        there = dst.at[:, pl.ds(col_k, D)]
        pltpu.make_async_copy(
            osend.at[i, pl.ds(pl.multiple_of(h * TOK, TOK), TOK)], there, grad_recv.at[i]
        ).start()
        for dz, dk in peers:
            p = head_dev(dz, dk)
            pltpu.make_async_remote_copy(
                src_ref=osend.at[i, pl.ds(pl.multiple_of(p * TOK, TOK), TOK)], dst_ref=there,
                send_sem=grad_send.at[i], recv_sem=grad_recv.at[i], device_id=(c, p), device_id_type=MESH,
            ).start()

    for i, dst in enumerate((att_ref, dq_ref)):
        arrived(dst, out_recv.at[i])
    for i, dst in enumerate((dk_ref, dv_ref)):
        arrived(dst, grad_recv.at[i])
    sent = len(peers) * TOK
    for i in range(2):
        arrived(osend.at[i, pl.ds(0, sent)], grad_send.at[i])
        arrived(att_ref.at[:, pl.ds(0, len(peers) * BLK)], out_send.at[i])
        arrived(att_ref.at[:, pl.ds(0, len(peers) * BLK)], qg_send.at[i])
        for j in range(2):

            @pl.when(c >= j + 1)
            def _():
                arrived(hsend.at[j, i], part_send.at[j, i])

            @pl.when(has_after if j == 0 else has_before & has_after & (c != seam - 1))
            def _():
                for r in range(2):
                    arrived(chunk(i, r, 2 - j), halo_send.at[j, i, r])

        @pl.when(c == seam - 2)
        def _():
            for r in range(2):
                arrived(chunk(i, r, 2), extra_send.at[i, r])

    @pl.when(has_after)
    def _():
        arrived(docw.at[1], doc_send.at[0])

    @pl.when(has_before & has_after)
    def _():
        arrived(docw.at[1], doc_send.at[1])

    @pl.when(c >= last - 1)
    def _():
        for r in range(2):
            arrived(way(r), relay_send.at[r])


    arrived(kv.at[:, pl.ds(0, sent)], kv_send)


def hand_over(*refs):
    sources, targets, sems = refs[:4], refs[4:8], refs[8]
    copies = [pltpu.make_async_copy(sources[i], targets[i], sems.at[i]) for i in range(4)]
    for copy in copies:
        copy.start()
    for copy in copies:
        copy.wait()


def on_device(queries, stacked_keys, stacked_values, output_gradient, doc_ids):
    any_ref = pl.BlockSpec(memory_space=pl.ANY)
    dma = pltpu.SemaphoreType.DMA
    shapes = [jax.ShapeDtypeStruct(a.shape, a.dtype) for a in (queries, queries, stacked_keys, stacked_values)]
    results = pl.pallas_call(
        kernel,
        out_shape=[pltpu.VMEM(a.shape, a.dtype) for a in shapes],
        in_specs=[any_ref] * 5,
        out_specs=[any_ref] * 4,
        scratch_shapes=[
            pltpu.VMEM((2, WIN, D), jnp.bfloat16),
            pltpu.VMEM((4, 2, SL, BLK), jnp.bfloat16),
            pltpu.VMEM((3, 1, BLK), jnp.int32),
            pltpu.VMEM((4, 8, SL), jnp.int32),
            pltpu.VMEM((4, 2, SL, BLK), jnp.bfloat16),
            pltpu.VMEM((2, WIN, D), jnp.float32),
            pltpu.VMEM((2, 2, BLK, D), jnp.bfloat16),
            pltpu.VMEM((2, 2, BLK, D), jnp.bfloat16),
            pltpu.VMEM((2, BLK, D), jnp.bfloat16),
            pltpu.VMEM((2, BLK, D), jnp.bfloat16),
            pltpu.VMEM((4, KEYS, GRP * SL), jnp.bfloat16),
            dma, dma((2,)), dma((2,)), dma((4,)), dma((2, 2, 2)), dma((2, 2, 2)), dma((2,)), dma((2,)), dma,
            dma((2,)), dma((2,)), dma((2, 2)), dma((2, 2)), dma((2,)), dma((2,)),
            dma((2, 2)), dma((3,)), dma((3,)), pltpu.SemaphoreType.REGULAR,
        ],
        compiler_params=pltpu.CompilerParams(
            collective_id=0, has_side_effects=True, vmem_limit_bytes=60 * 2**20
        ),
    )(queries, stacked_keys, stacked_values, output_gradient, doc_ids.reshape(1, -1))
    return pl.pallas_call(
        hand_over, out_shape=shapes, in_specs=[any_ref] * 4, out_specs=[any_ref] * 4,
        scratch_shapes=[dma((4,))],
        compiler_params=pltpu.CompilerParams(vmem_limit_bytes=16 * 2**20),
    )(*results)


def solution(mesh):
    tokens = P(("ctx", "head"), None)
    return jax.shard_map(
        on_device, mesh=mesh, in_specs=(tokens,) * 4 + (P("ctx"),), out_specs=(tokens,) * 4, check_vma=False
    )
```

```python
import math

import jax
import jax.numpy as jnp
from jax import lax
from jax.experimental import pallas as pl
from jax.experimental.pallas import tpu as pltpu
from jax.sharding import PartitionSpec as P

D = 128
TOK = 64
SL = 128
BLK = 512
HALF = 256
WIN = 1536
KEYS = 1152
GRP = 4
MESH = pl.DeviceIdType.MESH
SCALE = 1.0 / math.sqrt(D)
LOG2E = 1.4426950408889634


def nt(a, b):
    return lax.dot_general(a, b, (((1,), (1,)), ((), ())), preferred_element_type=jnp.float32)


def tn(a, b):
    return lax.dot_general(a, b, (((0,), (0,)), ((), ())), preferred_element_type=jnp.float32)


def kernel(
    q_ref, k_ref, v_ref, g_ref, doc_ref,
    att_ref, dq_ref, dk_ref, dv_ref,
    kv, qg, docw, startb, outb, acc, hsend, hrecv, osend, relay, probs,
    kv_send, kv_recv, qg_send, qg_recv, halo_send, halo_recv, doc_send, doc_recv, own_sem,
    out_send, out_recv, part_send, part_recv, grad_send, grad_recv, extra_send, relay_send, relay_recv, go_sem,
):
    n_ctx = lax.axis_size("ctx")
    c = lax.axis_index("ctx")
    h = lax.axis_index("head")
    zh = h // 2
    core = lax.rem(h, 2)

    def head_dev(dz, dk):
        return lax.rem(zh + dz, 4) * 2 + lax.rem(core + dk, 2)

    last, seam = n_ctx - 1, n_ctx // 2

    peers = [(0, 1), (1, 0), (1, 1), (3, 0), (3, 1), (2, 0), (2, 1)]

    own_row = pl.multiple_of(2 * BLK + h * TOK, TOK)
    col_q = pl.multiple_of(h * BLK, BLK)
    col_k = pl.multiple_of(h * D, D)
    tok_row = pl.multiple_of(core * TOK, TOK)

    @pl.when(c < 2)
    def _():
        kv[:, : 2 * BLK] = jnp.zeros((2, 2 * BLK, D), jnp.bfloat16)
        docw[0] = jnp.full((1, BLK), -1, jnp.int32)
        docw[1] = jnp.full((1, BLK), -1, jnp.int32)

    @pl.when((c == 0) | (c == seam - 1) | (c == last))
    def _():
        hrecv[...] = jnp.zeros_like(hrecv)

    barrier = pltpu.get_barrier_semaphore()
    for dz, dk in peers:
        pl.semaphore_signal(barrier, inc=1, device_id=(c, head_dev(dz, dk)), device_id_type=MESH)
    has_before, has_after = c >= 1, c < last
    turning = ((c >= seam - 2) & (c <= seam)) | (c >= last - 1)
    near = [(has_before, c - 1), (has_after, c + 1)]
    for other in (seam - 2, seam - 1, seam, last - 1, last):
        near.append((turning & ((c < other - 1) | (c > other + 1)), other))
    partners = len(peers)
    for there, other in near:
        partners = partners + jnp.where(there, 1, 0)

        @pl.when(there)
        def _():
            pl.semaphore_signal(barrier, inc=1, device_id=(other, h), device_id_type=MESH)

    for i, src in enumerate((k_ref, v_ref)):
        pltpu.make_async_copy(src.at[:, pl.ds(col_k, D)], kv.at[i, pl.ds(own_row, TOK)], kv_recv.at[i]).start()
    for i, src in enumerate((q_ref, g_ref)):
        pltpu.make_async_copy(
            src.at[:, pl.ds(col_q, BLK)], qg.at[zh, i, pl.ds(tok_row, TOK)], qg_recv.at[zh]
        ).start()
    pltpu.make_async_copy(doc_ref, docw.at[2], own_sem).start()
    pl.semaphore_wait(barrier, partners)

    for i, src in enumerate((k_ref, v_ref)):
        for dz, dk in reversed(peers):
            p = head_dev(dz, dk)
            pltpu.make_async_remote_copy(
                src_ref=src.at[:, pl.ds(pl.multiple_of(p * D, D), D)],
                dst_ref=kv.at[i, pl.ds(own_row, TOK)],
                send_sem=kv_send, recv_sem=kv_recv.at[i], device_id=(c, p), device_id_type=MESH,
            ).start()

    after, before = (c + 1, h), (c - 1, h)

    def pass_on(src, dst, send_sem, recv_sem, to=after):
        pltpu.make_async_remote_copy(
            src_ref=src, dst_ref=dst, send_sem=send_sem, recv_sem=recv_sem, device_id=to, device_id_type=MESH
        ).start()

    def arrived(ref, sem):
        pltpu.make_async_copy(ref, ref, sem).wait()

    def chunk(i, r, block):
        return kv.at[i, pl.ds(block * BLK + r * HALF, HALF)]

    for dz, dk in peers[:5]:
        p = head_dev(dz, dk)
        for i, src in enumerate((q_ref, g_ref)):
            pltpu.make_async_remote_copy(
                src_ref=src.at[:, pl.ds(pl.multiple_of(p * BLK, BLK), BLK)],
                dst_ref=qg.at[zh, i, pl.ds(tok_row, TOK)],
                send_sem=qg_send.at[i], recv_sem=qg_recv.at[zh], device_id=(c, p), device_id_type=MESH,
            ).start()

    def way(r):
        return relay.at[0, pl.ds(r * HALF, HALF)]

    @pl.when(has_after)
    def _():
        pass_on(doc_ref, docw.at[1], doc_send.at[0], doc_recv.at[0])

    for i in range(2):
        arrived(kv.at[i, pl.ds(2 * BLK, BLK)], kv_recv.at[i])

        @pl.when(has_after & ((c != seam - 1) | (i == 1)))
        def _():
            for r in range(2):
                pass_on(chunk(i, r, 2), chunk(i, r, 1), halo_send.at[0, i, r], halo_recv.at[0, i, r])

        @pl.when((c == seam - 1) & (i == 0))
        def _():
            for r in range(2):
                pass_on(chunk(i, r, 2), way(r), halo_send.at[0, i, r], relay_recv.at[r], (last, h))

        @pl.when(c == seam - 2)
        def _():
            for r in range(2):
                if i == 0:
                    pass_on(chunk(i, r, 2), chunk(i, r, 0), extra_send.at[i, r], halo_recv.at[1, i, r], (seam, h))
                else:
                    pass_on(chunk(i, r, 2), way(r), extra_send.at[i, r], relay_recv.at[r], (last - 1, h))

    for dz, dk in peers[5:]:
        p = head_dev(dz, dk)
        for i, src in enumerate((q_ref, g_ref)):
            pltpu.make_async_remote_copy(
                src_ref=src.at[:, pl.ds(pl.multiple_of(p * BLK, BLK), BLK)],
                dst_ref=qg.at[zh, i, pl.ds(tok_row, TOK)],
                send_sem=qg_send.at[i], recv_sem=qg_recv.at[zh], device_id=(c, p), device_id_type=MESH,
            ).start()

    def turn(where, i, stage):
        @pl.when(c == where)
        def _():
            for r in range(2):
                arrived(way(r), relay_recv.at[r])
                pass_on(way(r), chunk(i, r, 1 - stage), relay_send.at[r], halo_recv.at[stage, i, r], (seam, h))

    turn(last, 0, 0)

    @pl.when(has_before)
    def _():
        arrived(docw.at[1], doc_recv.at[0])

        @pl.when(has_after)
        def _():
            pass_on(docw.at[1], docw.at[0], doc_send.at[1], doc_recv.at[1])

        for i in range(2):
            for r in range(2):
                arrived(chunk(i, r, 1), halo_recv.at[0, i, r])

                @pl.when(has_after & (c != seam - 1))
                def _():
                    pass_on(chunk(i, r, 1), chunk(i, r, 0), halo_send.at[1, i, r], halo_recv.at[1, i, r])

    turn(last - 1, 1, 1)
    acc[...] = jnp.zeros_like(acc)
    pltpu.make_async_copy(doc_ref, docw.at[2], own_sem).wait()

    @pl.when(c >= 2)
    def _():
        arrived(docw.at[0], doc_recv.at[1])

    docs = jnp.concatenate([docw[0], docw[1], docw[2]], axis=1)
    lane = lax.broadcasted_iota(jnp.int32, (1, WIN), 1)
    docs = jnp.where(lane + (c - 2) * BLK >= 0, docs, -1)
    docs = jnp.broadcast_to(docs, (8, WIN))
    lane = lax.broadcasted_iota(jnp.int32, (8, WIN), 1)
    begins = jnp.where((lane == 0) | (docs != pltpu.roll(docs, 1, 1)), lane, 0)
    step = 1
    while step < WIN:
        begins = jnp.maximum(begins, jnp.where(lane >= step, pltpu.roll(begins, step, 1), 0))
        step *= 2
    for s in range(4):
        startb[s] = begins[:, 2 * BLK + s * SL : 2 * BLK + (s + 1) * SL]

    def earliest(i):
        @pl.when(c >= 2)
        def _():
            for r in range(2):
                arrived(chunk(i, r, 0), halo_recv.at[1, i, r])

    def stacked(s, which):
        return jnp.concatenate([qg[s, which, :, i * D : (i + 1) * D] for i in range(GRP)], axis=0)

    def weigh(s):
        arrived(qg.at[s], qg_recv.at[s])
        first = pl.multiple_of(s * SL, SL)
        q4 = stacked(s, 0)
        start = startb[s][0:1]
        start = jnp.concatenate([start] * GRP, axis=1) - first
        early, late = 2 * BLK, SL
        row = lax.broadcasted_iota(jnp.int32, (early, GRP * SL), 0)
        far = nt(kv[0, pl.ds(first, early)], q4) * (SCALE * LOG2E)
        far = jnp.where(row >= start, far, -jnp.inf)
        row = lax.broadcasted_iota(jnp.int32, (late, GRP * SL), 0)
        column = lax.rem(lax.broadcasted_iota(jnp.int32, (1, GRP * SL), 1), SL)
        close = nt(kv[0, pl.ds(pl.multiple_of(first + early, SL), late)], q4) * (SCALE * LOG2E)
        close = jnp.where((row >= start - early) & (row <= column), close, -jnp.inf)
        peak = jnp.maximum(jnp.max(far, axis=0, keepdims=True), jnp.max(close, axis=0, keepdims=True))
        far, close = jnp.exp2(far - peak), jnp.exp2(close - peak)
        part = 1.0 / (jnp.sum(far, axis=0, keepdims=True) + jnp.sum(close, axis=0, keepdims=True))
        probs[s, :early] = (far * part).astype(jnp.bfloat16)
        probs[s, early:] = (close * part).astype(jnp.bfloat16)

    def send_back(s, i):
        dst = (att_ref, dq_ref)[i]
        for cc in range(2):
            piece = outb.at[s, i, pl.ds(cc * TOK, TOK)]
            there = dst.at[:, pl.ds(col_q, BLK)]

            @pl.when(2 * s + cc == h)
            def _():
                pltpu.make_async_copy(piece, there, out_recv.at[i]).start()

            @pl.when(2 * s + cc != h)
            def _():
                pltpu.make_async_remote_copy(
                    src_ref=piece, dst_ref=there, send_sem=out_send.at[i], recv_sem=out_recv.at[i],
                    device_id=(c, 2 * s + cc), device_id_type=MESH,
                ).start()

    def weigh_near(j, carry):
        weigh(lax.rem(zh + jnp.where(j == 2, 3, j), 4))
        return carry

    def unit(j, carry):
        s = lax.rem(zh + jnp.where(j == 0, 1, jnp.where(j == 1, 3, jnp.where(j == 2, 0, 2))), 4)

        @pl.when(j == 3)
        def _():
            weigh(s)

        first = pl.multiple_of(s * SL, SL)
        values = kv[1, pl.ds(first, KEYS)]
        weights = probs[s]
        g4 = stacked(s, 1)
        att = tn(values, weights).astype(jnp.bfloat16).astype(jnp.float32)
        for i in range(GRP):
            outb[s, 0, :, i * D : (i + 1) * D] = jnp.transpose(att[:, i * D : (i + 1) * D]).astype(jnp.bfloat16)
        send_back(s, 0)
        dot = jnp.sum(att * jnp.transpose(g4.astype(jnp.float32)), axis=0, keepdims=True)
        dscore = (weights.astype(jnp.float32) * (nt(values, g4) - dot)).astype(jnp.bfloat16)
        dq = tn(kv[0, pl.ds(first, KEYS)], dscore) * SCALE
        for i in range(GRP):
            outb[s, 1, :, i * D : (i + 1) * D] = jnp.transpose(dq[:, i * D : (i + 1) * D]).astype(jnp.bfloat16)
        send_back(s, 1)
        acc[0, pl.ds(first, KEYS)] += jnp.dot(dscore, stacked(s, 0), preferred_element_type=jnp.float32)
        acc[1, pl.ds(first, KEYS)] += jnp.dot(weights, g4, preferred_element_type=jnp.float32)
        return carry

    earliest(0)
    lax.fori_loop(0, 3, weigh_near, 0)
    earliest(1)

    @pl.when(c == 1)
    def _():
        pl.semaphore_signal(go_sem, inc=1, device_id=(0, h), device_id_type=MESH)

    @pl.when(c == 0)
    def _():
        pl.semaphore_wait(go_sem, 1)

    lax.fori_loop(0, 4, unit, 0)

    factors = (SCALE, 1.0)

    def give(stage, i):
        here, sent = hsend.at[stage, i], part_send.at[stage, i]

        @pl.when((c >= stage + 1) & (c != (seam if stage == 1 else -1)))
        def _():
            pass_on(here, hrecv.at[stage, i], sent, part_recv.at[stage, i], before)

        if stage == 1:

            @pl.when(c == seam)
            def _():
                pass_on(here, relay.at[i], sent, relay_recv.at[i], (seam - 2, h))

    for i in range(2):
        hsend[1, i] = (acc[i, :BLK] * factors[i]).astype(jnp.bfloat16)
        give(1, i)
    for i in range(2):

        @pl.when(has_before & has_after & (c != seam - 1))
        def _():
            arrived(hrecv.at[1, i], part_recv.at[1, i])

        hsend[0, i] = (acc[i, BLK : 2 * BLK] * factors[i] + hrecv[1, i].astype(jnp.float32)).astype(jnp.bfloat16)
        give(0, i)
    for i, dst in enumerate((dk_ref, dv_ref)):

        @pl.when(has_after)
        def _():
            arrived(hrecv.at[0, i], part_recv.at[0, i])

        mine = acc[i, 2 * BLK :] * factors[i]
        mine = mine + hrecv[0, i].astype(jnp.float32)


        @pl.when(c != seam - 2)
        def _():
            osend[i] = mine.astype(jnp.bfloat16)

        @pl.when(c == seam - 2)
        def _():
            arrived(relay.at[i], relay_recv.at[i])
            osend[i] = (mine + relay[i].astype(jnp.float32)).astype(jnp.bfloat16)

        there = dst.at[:, pl.ds(col_k, D)]
        pltpu.make_async_copy(
            osend.at[i, pl.ds(pl.multiple_of(h * TOK, TOK), TOK)], there, grad_recv.at[i]
        ).start()
        for dz, dk in reversed(peers):
            p = head_dev(dz, dk)
            pltpu.make_async_remote_copy(
                src_ref=osend.at[i, pl.ds(pl.multiple_of(p * TOK, TOK), TOK)], dst_ref=there,
                send_sem=grad_send.at[i], recv_sem=grad_recv.at[i], device_id=(c, p), device_id_type=MESH,
            ).start()

    for i, dst in enumerate((att_ref, dq_ref)):
        arrived(dst, out_recv.at[i])
    for i, dst in enumerate((dk_ref, dv_ref)):
        arrived(dst, grad_recv.at[i])
    sent = len(peers) * TOK
    for i in range(2):
        arrived(osend.at[i, pl.ds(0, sent)], grad_send.at[i])
        arrived(att_ref.at[:, pl.ds(0, len(peers) * BLK)], out_send.at[i])
        arrived(att_ref.at[:, pl.ds(0, len(peers) * BLK)], qg_send.at[i])
        for j in range(2):

            @pl.when(c >= j + 1)
            def _():
                arrived(hsend.at[j, i], part_send.at[j, i])

            @pl.when(has_after if j == 0 else has_before & has_after & (c != seam - 1))
            def _():
                for r in range(2):
                    arrived(chunk(i, r, 2 - j), halo_send.at[j, i, r])

        @pl.when(c == seam - 2)
        def _():
            for r in range(2):
                arrived(chunk(i, r, 2), extra_send.at[i, r])

    @pl.when(has_after)
    def _():
        arrived(docw.at[1], doc_send.at[0])

    @pl.when(has_before & has_after)
    def _():
        arrived(docw.at[1], doc_send.at[1])

    @pl.when(c >= last - 1)
    def _():
        for r in range(2):
            arrived(way(r), relay_send.at[r])


    arrived(kv.at[:, pl.ds(0, sent)], kv_send)


def hand_over(*refs):
    sources, targets, sems = refs[:4], refs[4:8], refs[8]
    copies = [pltpu.make_async_copy(sources[i], targets[i], sems.at[i]) for i in range(4)]
    for copy in copies:
        copy.start()
    for copy in copies:
        copy.wait()


def on_device(queries, stacked_keys, stacked_values, output_gradient, doc_ids):
    any_ref = pl.BlockSpec(memory_space=pl.ANY)
    dma = pltpu.SemaphoreType.DMA
    shapes = [jax.ShapeDtypeStruct(a.shape, a.dtype) for a in (queries, queries, stacked_keys, stacked_values)]
    results = pl.pallas_call(
        kernel,
        out_shape=[pltpu.VMEM(a.shape, a.dtype) for a in shapes],
        in_specs=[any_ref] * 5,
        out_specs=[any_ref] * 4,
        scratch_shapes=[
            pltpu.VMEM((2, WIN, D), jnp.bfloat16),
            pltpu.VMEM((4, 2, SL, BLK), jnp.bfloat16),
            pltpu.VMEM((3, 1, BLK), jnp.int32),
            pltpu.VMEM((4, 8, SL), jnp.int32),
            pltpu.VMEM((4, 2, SL, BLK), jnp.bfloat16),
            pltpu.VMEM((2, WIN, D), jnp.float32),
            pltpu.VMEM((2, 2, BLK, D), jnp.bfloat16),
            pltpu.VMEM((2, 2, BLK, D), jnp.bfloat16),
            pltpu.VMEM((2, BLK, D), jnp.bfloat16),
            pltpu.VMEM((2, BLK, D), jnp.bfloat16),
            pltpu.VMEM((4, KEYS, GRP * SL), jnp.bfloat16),
            dma, dma((2,)), dma((2,)), dma((4,)), dma((2, 2, 2)), dma((2, 2, 2)), dma((2,)), dma((2,)), dma,
            dma((2,)), dma((2,)), dma((2, 2)), dma((2, 2)), dma((2,)), dma((2,)),
            dma((2, 2)), dma((3,)), dma((3,)), pltpu.SemaphoreType.REGULAR,
        ],
        compiler_params=pltpu.CompilerParams(
            collective_id=0, has_side_effects=True, vmem_limit_bytes=60 * 2**20
        ),
    )(queries, stacked_keys, stacked_values, output_gradient, doc_ids.reshape(1, -1))
    return pl.pallas_call(
        hand_over, out_shape=shapes, in_specs=[any_ref] * 4, out_specs=[any_ref] * 4,
        scratch_shapes=[dma((4,))],
        compiler_params=pltpu.CompilerParams(vmem_limit_bytes=16 * 2**20),
    )(*results)


def solution(mesh):
    tokens = P(("ctx", "head"), None)
    return jax.shard_map(
        on_device, mesh=mesh, in_specs=(tokens,) * 4 + (P("ctx"),), out_specs=(tokens,) * 4, check_vma=False
    )
```
